128 devices in a mesh: dp: 2 (over core), expert: 8 (over x_lo, z), etp: 8 (over x_hi, y).
Axes of the slice: x: 4 (x_hi: 2, x_lo: 2; x = x_hi * 2 + x_lo), y: 4, z: 4, core: 2. Of those that a mesh axis runs over, the one named last changes fastest.
Arguments:
- grad_out: bfloat16 [16384, 3072], P(('dp', 'expert', 'etp')), may hold values from -6 to 6
- expert_ids: int32 [16384, 2], P(('dp', 'expert', 'etp')), may hold values from 0 to 7, all different within a row; in each aligned block of 128 rows (0 to 127, 128 to 255, ...) at most 36 rows name the same one
- gate_probs: bfloat16 [16384, 2], P(('dp', 'expert', 'etp')), may hold values from 0.099609375 to 0.8984375
- keep_mask: int32 [16384, 2], P(('dp', 'expert', 'etp')), may hold values 0 or 1
- pre_gate: bfloat16 [8, 4608, 8192], P('expert', 'dp', 'etp'), may hold values from -4 to 4
- pre_up: bfloat16 [8, 4608, 8192], P('expert', 'dp', 'etp'), may hold values from -4 to 4
- w_down: bfloat16 [8, 8192, 3072], P('expert', 'etp', 'dp'), may hold values from -0.0625 to 0.0625
Outputs:
- grad_pre_gate: bfloat16 [8, 4608, 8192], P('expert', 'dp', 'etp')
- grad_pre_up: bfloat16 [8, 4608, 8192], P('expert', 'dp', 'etp')
- grad_w_down: bfloat16 [8, 8192, 3072], P('expert', 'etp', 'dp')
- grad_gate_probs: float32 [16384, 2], P(('dp', 'expert', 'etp'))
The draws below stay inside these ranges and needn't reach their ends.
Inputs may be any that keep to these rules, and one draw needn't show every extreme that they name: `expert_ids`: the two experts of a token differ. Among the 128 tokens of one device no expert is chosen more than 36 times, and on some devices one expert is chosen exactly 36 times.
All inputs are finite; a program needn't handle non-finite values. No bound on the sum of `keep_mask` on one device may be relied on, other than what follows from the above.
Results may differ from the reference program's by a relative error of at most 0.0058.
Values may be sent and summed in bfloat16 or wider, within the bound.
No kernel may reach another device: no remote copies, remote signals or barrier semaphores. Data moves between devices by JAX's collectives and lax.ppermute only.
A program may use at most 192 MiB of HBM per device.

```python
import math
import jax
import jax.numpy as jnp
import numpy as np
from jax import lax

D = 3072
FF = 8192
TOK_DEV = 128
EXPERTS = 8
CAP = 36
TOKENS = 16384
SLOTS = 4608
N_DP = 2
N_EXPERT = 8
N_ETP = 8


def touch_ends(values, key, smallest, top_value):
    longest = values.shape.index(max(values.shape))
    spots = []
    for shift in (0, 1):
        where = [jax.random.randint(jax.random.fold_in(key, axis), (), 0, length) for axis, length in enumerate(values.shape)]
        where[longest] = (where[longest] + shift) % values.shape[longest]
        spots.append(tuple(where))
    return values.at[spots[0]].set(smallest).at[spots[1]].set(top_value)


def block_levels(rng, dims, split, smallest, high):
    loudness, own = 1.0, jax.random.fold_in(rng, 6)
    for dim, parts in split:
        heights = jnp.exp(jax.random.uniform(jax.random.fold_in(own, dim), (parts,), jnp.float32, smallest / len(split), high / len(split)))
        loudness = loudness * jnp.repeat(heights, dims[dim] // parts).reshape([-1 if axis == dim else 1 for axis in range(len(dims))])
    return loudness


def routed_block(stream_key, own, number, rows, amount, top, most, slope):
    sequence = jax.random.permutation(stream_key, amount)
    heavy_load, common = portions_of(amount, rows * top, most, slope, True), portions_of(amount, rows * top, most, slope, False)
    places = jnp.arange(amount)

    def named(sizes, offset_by):
        used = int((sizes > 0).sum())
        fixed = max(1, used // 4)
        passed = fixed + (places - fixed + offset_by * (used - fixed)) % max(1, amount - fixed)
        return jnp.zeros((amount,), jnp.int32).at[sequence[jnp.where(places < fixed, places, passed)]].set(jnp.asarray(sizes, jnp.int32))

    sizes = jnp.where(number % 4 == 0, named(heavy_load, number // 4), named(common, number - number // 4 - 1))
    mixed = jax.random.permutation(jax.random.fold_in(own, 3), amount)
    source_of, sink = mixed[0:amount // 2 * 2:2], mixed[1:amount // 2 * 2:2]
    room = jnp.minimum(sizes[source_of] - 1, most - sizes[sink]) // 2
    room = jnp.where((source_of == sequence[0]) | (sink == sequence[0]) | (sizes[sink] == 0), 0, jnp.maximum(room, 0))
    passed = jax.random.randint(jax.random.fold_in(own, 4), (amount // 2,), 0, 1 << 20) % (room + 1)
    sizes = sizes.at[source_of].add(-passed).at[sink].add(passed)
    labels = jnp.searchsorted(jnp.cumsum(sizes), jnp.arange(rows * top), side="right").astype(jnp.int32)
    listing = labels.reshape(top, rows).T
    listing = listing[jax.random.permutation(jax.random.fold_in(own, 1), rows)]
    offset_by = jax.random.randint(jax.random.fold_in(own, 2), (rows, 1), 0, top)
    return jnp.take_along_axis(listing, (jnp.arange(top)[None, :] + offset_by) % top, axis=1)


def portions_of(number_of, total, bound, lean, full):
    loads = [(1 << 20) // math.isqrt(grade ** lean) + 1 for grade in range(1, number_of + 1)]
    largest = bound if full else min(bound, max(-(-total // number_of), total * loads[0] // sum(loads)))
    least = 1 if total - largest >= number_of - 1 else 0
    holding, rest = [largest] + [least] * (number_of - 1), total - largest - least * (number_of - 1)
    while rest > 0:
        candidates = [i for i in range(1, number_of) if holding[i] < largest] or [i for i in range(1, number_of) if holding[i] < bound]
        pool, left = sum([loads[i] for i in candidates]), rest
        for i in candidates:
            extra = min(bound - holding[i], max(1, left * loads[i] // pool), rest)
            holding[i] = holding[i] + extra
            rest = rest - extra
    return np.array(holding)


def scatter_about(own_key, shape, scale, most, pieces=(), kind=jnp.bfloat16):
    drawn = jax.random.normal(own_key, shape, jnp.float32) * scale
    if len(pieces) > 0:
        drawn = block_levels(own_key, shape, pieces, -0.22, 0.18) * drawn
    return jnp.clip(drawn, min=-most, max=most).astype(kind)


def setup_inputs(seed: int = 0) -> dict:
    arg_keys = jax.random.split(jax.random.key(seed), 8)
    grad_out = scatter_about(arg_keys[0], (TOKENS, D), 1.0, 6.0, ((0, 128),))
    expert_ids_keys = jax.random.split(jax.random.fold_in(arg_keys[1], 1), TOKENS // TOK_DEV)
    expert_ids_turns = jax.random.permutation(jax.random.fold_in(arg_keys[1], 3), TOKENS // TOK_DEV)
    expert_ids = jax.vmap(lambda own, number: routed_block(jax.random.fold_in(arg_keys[1], 2), own, number, TOK_DEV, EXPERTS, 2, CAP, 2))(expert_ids_keys, expert_ids_turns).reshape((TOKENS, 2))
    gate_probs = jnp.clip(0.099609375 + 0.7988281 * jax.random.uniform(arg_keys[2], (TOKENS, 2), jnp.float32) ** block_levels(arg_keys[2], (TOKENS, 2), ((0, 128),), -0.2, 0.2), 0.099609375, 0.8984375).astype(jnp.bfloat16)
    keep_mask = touch_ends((jax.random.randint(arg_keys[3], (TOKENS, 2), 0, 4) < 3).astype(jnp.int32), jax.random.fold_in(arg_keys[3], 1), 0, 1)
    pre_gate = scatter_about(arg_keys[4], (EXPERTS, SLOTS, FF), 1.0, 4.0, ((0, 8), (1, 2), (2, 8)))
    pre_up = scatter_about(arg_keys[5], (EXPERTS, SLOTS, FF), 1.0, 4.0, ((0, 8), (1, 2), (2, 8)))
    w_down = scatter_about(arg_keys[6], (EXPERTS, FF, D), FF ** -0.5, 0.0625, ((0, 8), (1, 8), (2, 2)))
    return dict(grad_out=grad_out, expert_ids=expert_ids, gate_probs=gate_probs, keep_mask=keep_mask, pre_gate=pre_gate, pre_up=pre_up, w_down=w_down)


def expert_backward(operands):
    grad_rows, gate_rows, gate_pre, up_pre, down_proj = operands
    back_full = jnp.dot(grad_rows, down_proj.T, preferred_element_type=jnp.float32)
    pre_gate = gate_pre.astype(jnp.float32)
    pre_up = up_pre.astype(jnp.float32)
    sigmoid_gate = jax.nn.sigmoid(pre_gate)
    swish_gate = pre_gate * sigmoid_gate
    product = swish_gate * pre_up
    hidden_act = product.astype(jnp.bfloat16)
    gate_float = gate_rows.astype(jnp.float32)[:, None]
    upstream = gate_float * back_full
    grad_gate = (upstream * pre_up * (sigmoid_gate * (1.0 + pre_gate * (1.0 - sigmoid_gate)))).astype(jnp.bfloat16)
    grad_upper = (upstream * swish_gate).astype(jnp.bfloat16)
    scaled = (gate_float * grad_rows.astype(jnp.float32)).astype(jnp.bfloat16)
    wgrad_down = jnp.dot(hidden_act.T, scaled, preferred_element_type=jnp.float32).astype(jnp.bfloat16)
    gate_term = jnp.sum(product * back_full, axis=1)
    return grad_gate, grad_upper, wgrad_down, gate_term


def reference(grad_out, expert_ids, gate_probs, keep_mask, pre_gate, pre_up, w_down):
    blocks = N_DP * N_EXPERT * N_ETP
    block_ids = expert_ids.reshape(blocks, 2 * TOK_DEV)
    onehot = (block_ids[:, :, None] == jnp.arange(EXPERTS, dtype=jnp.int32)[None, None, :]).astype(jnp.int32)
    before = jnp.cumsum(onehot, axis=1) - onehot
    slot_index = jnp.sum(before * onehot, axis=2)
    target = (jnp.arange(blocks, dtype=jnp.int32)[:, None] * CAP + slot_index).reshape(-1).astype(jnp.int32)
    flat_ids = expert_ids.reshape(-1).astype(jnp.int32)
    kept_gate = (gate_probs * keep_mask.astype(gate_probs.dtype)).reshape(-1)
    grad_slots = jnp.zeros((EXPERTS, SLOTS, D), grad_out.dtype).at[flat_ids, target].set(jnp.repeat(grad_out, 2, axis=0))
    gate_slots = jnp.zeros((EXPERTS, SLOTS), gate_probs.dtype).at[flat_ids, target].set(kept_gate)
    grad_gate, grad_upper, wgrad_down, gate_term = lax.map(expert_backward, (grad_slots, gate_slots, pre_gate, pre_up, w_down))
    picked = gate_term[flat_ids, target].reshape(TOKENS, 2)
    grad_gate_probs = keep_mask.astype(jnp.float32) * picked
    return grad_gate, grad_upper, wgrad_down, grad_gate_probs
```

```python
import functools

import jax
import jax.numpy as jnp
from jax import lax
from jax.experimental import pallas as pl
from jax.experimental.pallas import tpu as pltpu
from jax.sharding import PartitionSpec as P

AXES = ("dp", "expert", "etp")
EXPERTS = 8
CAP = 36
TOK = 128
D = 3072
HALF = 1536
FF = 1024
ROWS = 2304
PAIR = 2 * CAP
UNIT = 4 * CAP
FT = 256
VMEM = 56 * 1024 * 1024


def position(flat):
    dp, rest = divmod(flat, 64)
    expert, etp = divmod(rest, 8)
    x_lo, z = divmod(expert, 4)
    x_hi, y = divmod(etp, 4)
    return dp, x_hi * 2 + x_lo, y, z


def flat_of(dp, x, y, z):
    return dp * 64 + ((x % 2) * 4 + z) * 8 + (x // 2) * 4 + y


def move(array, step):
    pairs = []
    for source in range(128):
        dp, x, y, z = position(source)
        pairs.append((source, flat_of(*step(dp, x, y, z))))
    return lax.ppermute(array, AXES, pairs)


def along_x(k):
    return lambda dp, x, y, z: (dp, (x + k) % 4, y, z)


def along_z(k):
    return lambda dp, x, y, z: (dp, x, y, (z + k) % 4)


def turned(dp, y, change):
    return (change((y - dp) % 4) + dp) % 4


def near_pair(dp, x, y, z):
    return dp, x, turned(dp, y, lambda v: v ^ 1), z


def far_pair(dp, x, y, z):
    return dp, x, turned(dp, y, lambda v: 3 - v), z


def other_core(dp, x, y, z):
    return 1 - dp, x, y, z


def slot_lines(meta):
    names = lax.broadcasted_iota(jnp.int32, (EXPERTS, TOK), 0).astype(jnp.float32)
    first = (names == meta[0:1, :]).astype(jnp.float32)
    second = (names == meta[1:2, :]).astype(jnp.float32)
    row = lax.broadcasted_iota(jnp.int32, (TOK, TOK), 0)
    col = lax.broadcasted_iota(jnp.int32, (TOK, TOK), 1)
    earlier = (row < col).astype(jnp.bfloat16)
    before = jnp.dot(
        (first + second).astype(jnp.bfloat16), earlier, preferred_element_type=jnp.float32
    )
    return (
        jnp.sum(before * first, axis=0, keepdims=True),
        jnp.sum(before * second, axis=0, keepdims=True),
    )


def slots_kernel(sp, own_meta, par_meta, own_x, par_x, s0, s1, s2, s3, slot_out):
    z, x_lo, odd = sp[0], sp[1], sp[2]
    own_slots = slot_lines(own_meta[...])
    par_slots = slot_lines(par_meta[...])
    slot_out[...] = jnp.concatenate(
        [own_slots[0], own_slots[1], jnp.zeros((6, TOK), jnp.float32)], axis=0
    )
    row = lax.broadcasted_iota(jnp.int32, (UNIT, 1), 0)
    other = row >= PAIR
    within = jnp.where(other, row - PAIR, row)
    late = (within >= CAP).astype(jnp.int32)
    slot = jnp.where(within >= CAP, within - CAP, within).astype(jnp.float32)
    lo = jnp.where(other, 1 - x_lo, x_lo)
    for k, out in enumerate((s0, s1, s2, s3)):
        z_to = lax.rem(z + k, 4)
        expert = (lo * 4 + z_to).astype(jnp.float32)
        total = jnp.zeros((UNIT, own_x.shape[1]), jnp.float32)
        for mine, meta, slots, x in (
            (True, own_meta, own_slots, own_x),
            (False, par_meta, par_slots, par_x),
        ):
            here = late == (odd if mine else 1 - odd)
            pick = jnp.zeros((UNIT, TOK), jnp.float32)
            for j in range(2):
                hit = (meta[j : j + 1, :] == expert) & (slots[j] == slot) & here
                pick = pick + jnp.where(hit, meta[2 + j : 3 + j, :], 0.0)
            total = total + jnp.dot(
                pick.astype(jnp.bfloat16), x[...], preferred_element_type=jnp.float32
            )
        out[...] = total.astype(jnp.bfloat16)


def build_slots(sp, own_meta, par_meta, own_x, par_x):
    tile = 1024
    whole = pl.BlockSpec((8, TOK), lambda i, sp: (0, 0))
    tokens = pl.BlockSpec((TOK, tile), lambda i, sp: (0, i))
    return pl.pallas_call(
        slots_kernel,
        grid_spec=pltpu.PrefetchScalarGridSpec(
            num_scalar_prefetch=1,
            grid=(D // tile,),
            in_specs=[whole, whole, tokens, tokens],
            out_specs=[pl.BlockSpec((UNIT, tile), lambda i, sp: (0, i))] * 4 + [whole],
        ),
        out_shape=[jax.ShapeDtypeStruct((UNIT, D), jnp.bfloat16)] * 4
        + [jax.ShapeDtypeStruct((8, TOK), jnp.float32)],
        cost_estimate=pl.CostEstimate(
            flops=2 * 4 * UNIT * 2 * TOK * D, bytes_accessed=6_000_000, transcendentals=0
        ),
        compiler_params=pltpu.CompilerParams(vmem_limit_bytes=VMEM),
    )(sp, own_meta, par_meta, own_x, par_x)


def chunk_kernel(first, last, sp, *refs):
    own_y, par_y, own_w, oth_w, gate, up = refs[:6]
    refs = refs[6:]
    if not first:
        sums_in, refs = refs[:2], refs[5:]
    grad_gate, grad_up, term, sums = refs[0], refs[1], refs[2], refs[3:5]
    back_s, hid_s, term_s = refs[5:]
    f = pl.program_id(0)
    mine = pl.ds(pl.multiple_of(sp[11], 128), HALF)
    others = pl.ds(pl.multiple_of(sp[12], 128), HALF)
    nt = (((1,), (1,)), ((), ()))
    tn = (((0,), (0,)), ((), ()))
    for side, y in enumerate((own_y, par_y)):
        back = lax.dot_general(y[:, mine], own_w[...], nt, preferred_element_type=jnp.float32)
        back = back + lax.dot_general(
            y[:, others], oth_w[...], nt, preferred_element_type=jnp.float32
        )
        for j in range(4):
            start = pl.multiple_of(sp[1 + side * 4 + j], 8)
            back_s[pl.ds(start, PAIR), :] = back[j * PAIR : (j + 1) * PAIR]
    for unit in range(4):
        rows = pl.ds(unit * UNIT, UNIT)
        upstream = pltpu.roll(back_s[rows, :], sp[9], 0)
        half, part = unit // 2, pl.ds((unit % 2) * UNIT, UNIT)
        a = gate[half, 0, part, :].astype(jnp.float32)
        b = up[half, 0, part, :].astype(jnp.float32)
        s = jax.nn.sigmoid(a)
        swish = a * s
        product = swish * b
        grad_gate[half, 0, part, :] = (upstream * b * (s * (1.0 + a * (1.0 - s)))).astype(
            jnp.bfloat16
        )
        grad_up[half, 0, part, :] = (upstream * swish).astype(jnp.bfloat16)
        term_here = product * upstream
        term_here = term_here[:, 0:128] + term_here[:, 128:256]

        @pl.when(f == 0)
        def _():
            term_s[rows, :] = term_here

        @pl.when(f > 0)
        def _():
            term_s[rows, :] += term_here

        hid_s[rows, :] = pltpu.roll(product, sp[10], 0)

    @pl.when(f == pl.num_programs(0) - 1)
    def _():
        for half in range(2):
            term[half, 0, :, :] = jnp.sum(
                term_s[pl.ds(half * 2 * UNIT, 2 * UNIT), :], axis=1, keepdims=True
            )

    total = [None, None]
    for side, y in enumerate((own_y, par_y)):
        hidden = jnp.concatenate(
            [
                hid_s[pl.ds(pl.multiple_of(sp[1 + side * 4 + j], 8), PAIR), :]
                for j in range(4)
            ],
            axis=0,
        ).astype(jnp.bfloat16)
        for i, cols in enumerate((mine, others)):
            part = lax.dot_general(hidden, y[:, cols], tn, preferred_element_type=jnp.float32)
            total[i] = part if side == 0 else total[i] + part
    for i in range(2):
        if not first:
            total[i] = total[i] + sums_in[i][...]
        sums[i][...] = total[i].astype(sums[i].dtype)


def run_chunk(first, last, sp, own_y, par_y, own_w, oth_w, gate, up, sums, carried):
    pre = pl.BlockSpec((2, 1, 2 * UNIT, FT), lambda f, sp: (0, sp[0], 0, f))
    rows = pl.BlockSpec((4 * PAIR, D), lambda f, sp: (0, 0))
    weight = pl.BlockSpec((FT, HALF), lambda f, sp: (f, 0))
    in_specs = [rows, rows, weight, weight, pre, pre]
    operands = [own_y, par_y, own_w, oth_w, gate, up]
    aliases = {}
    if not first:
        in_specs += [weight, weight] + [pl.BlockSpec(memory_space=pl.ANY)] * 3
        operands += list(sums) + list(carried)
        aliases = {9: 0, 10: 1, 11: 2}
    shape = jax.ShapeDtypeStruct
    other_type = jnp.bfloat16 if last else jnp.float32
    out = pl.pallas_call(
        functools.partial(chunk_kernel, first, last),
        grid_spec=pltpu.PrefetchScalarGridSpec(
            num_scalar_prefetch=1,
            grid=(FF // FT,),
            in_specs=in_specs,
            out_specs=[
                pre,
                pre,
                pl.BlockSpec((2, 1, 2 * UNIT, 1), lambda f, sp: (0, sp[0], 0, 0)),
                weight,
                weight,
            ],
            scratch_shapes=[
                pltpu.VMEM((4 * UNIT, FT), jnp.float32),
                pltpu.VMEM((4 * UNIT, FT), jnp.float32),
                pltpu.VMEM((4 * UNIT, 128), jnp.float32),
            ],
        ),
        out_shape=[
            shape((2, 4, 2 * UNIT, FF), jnp.bfloat16),
            shape((2, 4, 2 * UNIT, FF), jnp.bfloat16),
            shape((2, 4, 2 * UNIT, 1), jnp.float32),
            shape((FF, HALF), jnp.float32),
            shape((FF, HALF), other_type),
        ],
        input_output_aliases=aliases,
        cost_estimate=pl.CostEstimate(
            flops=4 * 4 * UNIT * D * FF,
            bytes_accessed=30_000_000,
            transcendentals=4 * UNIT * FF,
        ),
        compiler_params=pltpu.CompilerParams(vmem_limit_bytes=VMEM),
    )(sp, *operands)
    return out[:3], out[3:]


def local(grad_out, expert_ids, gate_probs, keep_mask, pre_gate, pre_up, w_down):
    dp = lax.axis_index("dp")
    expert = lax.axis_index("expert")
    etp = lax.axis_index("etp")
    x_lo, z = expert // 4, expert % 4
    x_hi, y = etp // 4, etp % 4
    x = x_hi * 2 + x_lo
    turned_y = (y - dp) % 4

    par_x = move(grad_out, near_pair)
    own_w = w_down[0]
    kept = gate_probs * keep_mask.astype(jnp.bfloat16)
    meta = jnp.concatenate(
        [
            expert_ids.T.astype(jnp.float32),
            kept.T.astype(jnp.float32),
            jnp.zeros((4, TOK), jnp.float32),
        ],
        axis=0,
    )
    par_meta = move(meta, near_pair)
    oth_w = move(own_w, other_core)

    sp = jnp.stack([z, x_lo, turned_y % 2]).astype(jnp.int32)
    sent = build_slots(sp, meta, par_meta, grad_out, par_x)
    slots = sent[4]
    arrived = {0: sent[0]}
    for k in (1, 3, 2):
        arrived[k] = move(sent[k], along_z(k))

    gate = pre_gate.reshape(2, 4, 2 * UNIT, FF)
    up = pre_up.reshape(2, 4, 2 * UNIT, FF)
    pair = turned_y // 2
    carried, sums = None, None
    order = (0, 1, 3, 2)
    for n, k in enumerate(order):
        same, other = arrived[k][:PAIR], arrived[k][PAIR:]
        own_y = jnp.concatenate(
            [
                same,
                move(other, along_x(1)),
                move(other, along_x(-1)),
                move(same, along_x(2)),
            ],
            axis=0,
        )
        par_y = move(own_y, far_pair)
        starts = []
        for p in (pair, 1 - pair):
            for away in (0, 3, 1, 2):
                source = (x + away) % 4
                starts.append(((source % 2) * 2 + source // 2) * UNIT + p * PAIR)
        sp = jnp.stack(
            [(z - k) % 4]
            + starts
            + [dp * CAP, (UNIT - dp * CAP) % UNIT, dp * HALF, (1 - dp) * HALF]
        ).astype(jnp.int32)
        carried, sums = run_chunk(
            n == 0, n == 3, sp, own_y, par_y, own_w, oth_w, gate, up, sums, carried
        )
    grad_gate, grad_up, term = carried
    grad_w = (sums[0] + move(sums[1], other_core).astype(jnp.float32)).astype(jnp.bfloat16)

    returned = lax.all_to_all(
        term.reshape(64, CAP), ("expert", "etp"), split_axis=0, concat_axis=0, tiled=True
    )
    summed = returned.reshape(EXPERTS, 8, CAP).sum(axis=1)
    hit = (expert_ids.T[:, :, None, None] == jnp.arange(EXPERTS)[None, None, :, None]) & (
        slots[:2, :, None, None] == jnp.arange(CAP, dtype=jnp.float32)[None, None, None, :]
    )
    picked = jnp.sum(jnp.where(hit, summed[None, None], 0.0), axis=(2, 3)).T
    kept_only = keep_mask.astype(jnp.float32) * picked
    grad_gate_probs = kept_only / gate_probs.astype(jnp.float32)
    return (
        grad_gate.reshape(1, ROWS, FF),
        grad_up.reshape(1, ROWS, FF),
        grad_w[None],
        grad_gate_probs,
    )


def solution(mesh):
    tokens = P(("dp", "expert", "etp"), None)
    acts = P("expert", "dp", "etp")
    weight = P("expert", "etp", "dp")
    return jax.shard_map(
        local,
        mesh=mesh,
        in_specs=(tokens, tokens, tokens, tokens, acts, acts, weight),
        out_specs=(acts, acts, weight, tokens),
        check_vma=False,
    )
```

```python
import functools

import jax
import jax.numpy as jnp
from jax import lax
from jax.experimental import pallas as pl
from jax.experimental.pallas import tpu as pltpu
from jax.sharding import PartitionSpec as P

AXES = ("dp", "expert", "etp")
EXPERTS = 8
CAP = 36
TOK = 128
D = 3072
HALF = 1536
FF = 1024
ROWS = 2304
PAIR = 2 * CAP
UNIT = 4 * CAP
FT = 256
NTILE = 512
MIB = 1024 * 1024
NT = (((1,), (1,)), ((), ()))
TN = (((0,), (0,)), ((), ()))


def position(flat):
    dp, rest = divmod(flat, 64)
    expert, etp = divmod(rest, 8)
    x_lo, z = divmod(expert, 4)
    x_hi, y = divmod(etp, 4)
    return dp, x_hi * 2 + x_lo, y, z


def flat_of(dp, x, y, z):
    return dp * 64 + ((x % 2) * 4 + z) * 8 + (x // 2) * 4 + y


def move(array, step):
    pairs = []
    for source in range(128):
        dp, x, y, z = position(source)
        pairs.append((source, flat_of(*step(dp, x, y, z))))
    return lax.ppermute(array, AXES, pairs)


def along_x(k):
    return lambda dp, x, y, z: (dp, (x + k) % 4, y, z)


def along_z(k):
    return lambda dp, x, y, z: (dp, x, y, (z + k) % 4)


def turned(dp, y, change):
    return (change((y - dp) % 4) + dp) % 4


def near_pair(dp, x, y, z):
    return dp, x, turned(dp, y, lambda v: v ^ 1), z


def far_pair(dp, x, y, z):
    return dp, x, turned(dp, y, lambda v: 3 - v), z


def other_core(dp, x, y, z):
    return 1 - dp, x, y, z


def after(value, *others):
    return lax.optimization_barrier((value,) + others)[0]


def held(array):
    return pltpu.with_memory_space_constraint(array, pltpu.VMEM)


def outside(array):
    return pltpu.with_memory_space_constraint(array, pltpu.HBM)


def slot_lines(meta):
    names = lax.broadcasted_iota(jnp.int32, (EXPERTS, TOK), 0).astype(jnp.float32)
    first = (names == meta[0:1, :]).astype(jnp.float32)
    second = (names == meta[1:2, :]).astype(jnp.float32)
    row = lax.broadcasted_iota(jnp.int32, (TOK, TOK), 0)
    col = lax.broadcasted_iota(jnp.int32, (TOK, TOK), 1)
    earlier = (row < col).astype(jnp.bfloat16)
    before = jnp.dot(
        (first + second).astype(jnp.bfloat16), earlier, preferred_element_type=jnp.float32
    )
    return (
        jnp.sum(before * first, axis=0, keepdims=True),
        jnp.sum(before * second, axis=0, keepdims=True),
    )


def slots_kernel(sp, own_meta, par_meta, own_x, par_x, s0, s1, s2, s3, slot_out):
    z, x_lo, odd = sp[0], sp[1], sp[2]
    own_slots = slot_lines(own_meta[...])
    par_slots = slot_lines(par_meta[...])
    slot_out[...] = jnp.concatenate(
        [own_slots[0], own_slots[1], jnp.zeros((6, TOK), jnp.float32)], axis=0
    )
    row = lax.broadcasted_iota(jnp.int32, (UNIT, 1), 0)
    other = row >= PAIR
    within = jnp.where(other, row - PAIR, row)
    late = (within >= CAP).astype(jnp.int32)
    slot = jnp.where(within >= CAP, within - CAP, within).astype(jnp.float32)
    lo = jnp.where(other, 1 - x_lo, x_lo)
    picks = []
    for mine, meta, slots in ((True, own_meta, own_slots), (False, par_meta, par_slots)):
        here = late == (odd if mine else 1 - odd)
        rows = []
        for k in range(4):
            expert = (lo * 4 + lax.rem(z + k, 4)).astype(jnp.float32)
            pick = jnp.zeros((UNIT, TOK), jnp.float32)
            for j in range(2):
                hit = (meta[j : j + 1, :] == expert) & (slots[j] == slot) & here
                pick = pick + jnp.where(hit, meta[2 + j : 3 + j, :], 0.0)
            rows.append(pick)
        picks.append(jnp.concatenate(rows, axis=0).astype(jnp.bfloat16))
    step = 512
    for at in range(0, D, step):
        cols = slice(at, at + step)
        total = jnp.dot(picks[0], own_x[:, cols], preferred_element_type=jnp.float32)
        total += jnp.dot(picks[1], par_x[:, cols], preferred_element_type=jnp.float32)
        total = total.astype(jnp.bfloat16)
        for k, out in enumerate((s0, s1, s2, s3)):
            out[:, cols] = total[k * UNIT : (k + 1) * UNIT]


def build_slots(sp, own_meta, par_meta, own_x, par_x):
    vmem = pl.BlockSpec(memory_space=pltpu.VMEM)
    return pl.pallas_call(
        slots_kernel,
        in_specs=[pl.BlockSpec(memory_space=pltpu.SMEM)] + [vmem] * 4,
        out_specs=[vmem] * 5,
        out_shape=[jax.ShapeDtypeStruct((UNIT, D), jnp.bfloat16)] * 4
        + [jax.ShapeDtypeStruct((8, TOK), jnp.float32)],
        cost_estimate=pl.CostEstimate(flops=1, bytes_accessed=1, transcendentals=0),
        compiler_params=pltpu.CompilerParams(vmem_limit_bytes=16 * MIB),
    )(sp, own_meta, par_meta, held(own_x), held(par_x))


def padded(rows):
    return (rows + 15) // 16 * 16


def act_kernel(sizes, offset, first, last, sp, *refs):
    units = sum(sizes)
    ys, refs = refs[: 2 * len(sizes)], refs[2 * len(sizes) :]
    w_halves, gate, up, refs = refs[:2], refs[2], refs[3], refs[4:]
    if not first:
        refs = refs[3 if last else 5 :]
    grad_gate, grad_up, term, hid_out, rows_out = refs[:5]
    far_out, refs = (refs[5], refs[6:]) if last else (None, refs[5:])
    rows_s, hid, gate_s, up_s, ggate_s, gup_s, back_s, hid_s, sum_s, term_s = refs[:10]
    sem_in, sem_out, sem_t, sem_h, sem_r = refs[10:]
    places = [pl.multiple_of(sp[5 + i] * UNIT, UNIT) for i in range(units)]
    loads = []
    for i in range(units):
        rows = pl.ds(places[i], UNIT)
        loads.append(
            (
                pltpu.make_async_copy(gate.at[rows, :], gate_s.at[i], sem_in.at[i, 0]),
                pltpu.make_async_copy(up.at[rows, :], up_s.at[i], sem_in.at[i, 1]),
            )
        )
    for pair in loads:
        for copy in pair:
            copy.start()
    starts, at = [], 0
    for n, y in enumerate(ys):
        rows = y.shape[0]
        starts.append(at)
        for h in range(2):
            cols = pl.ds(pl.multiple_of(sp[3 + h], 128), HALF)
            rows_s[at : at + rows, h * HALF : (h + 1) * HALF] = y[:, cols]
        gap = padded(rows) - rows
        if gap:
            rows_s[at + rows : at + rows + gap, :] = jnp.zeros((gap, D), jnp.bfloat16)
        at += rows + gap
    turn = sp[2] > 0
    wide = pl.ds(offset, rows_s.shape[0])
    stores = [pltpu.make_async_copy(rows_s, rows_out.at[wide, :], sem_r.at[0])]
    if last:
        stores.append(
            pltpu.make_async_copy(rows_s.at[:, pl.ds(HALF, HALF)], far_out, sem_r.at[1])
        )
    for copy in stores:
        copy.start()

    def back_of(f):
        cols = pl.ds(f * FT, FT)
        return lax.dot_general(
            rows_s[:, :HALF], w_halves[0][cols, :], NT, preferred_element_type=jnp.float32
        ) + lax.dot_general(
            rows_s[:, HALF:], w_halves[1][cols, :], NT, preferred_element_type=jnp.float32
        )

    later = back_of(0)
    for f in range(FF // FT):
        cols = pl.ds(f * FT, FT)
        back_f, hid_f = back_s.at[f % 2], hid_s.at[f % 2]
        back = later
        base = 0
        for g, size in enumerate(sizes):
            for side in range(2):
                for j in range(size):
                    start = pl.multiple_of((base + j) * UNIT + sp[side], 8)
                    piece = starts[2 * g + side] + j * PAIR
                    back_f[pl.ds(start, PAIR), :] = back[piece : piece + PAIR]
            base += size
        if f + 1 < FF // FT:
            later = back_of(f + 1)
        for i in range(units):
            rows = pl.ds(i * UNIT, UNIT)
            if f == 0:
                for copy in loads[i]:
                    copy.wait()
            straight = back_f[rows, :]
            upstream = jnp.where(turn, pltpu.roll(straight, CAP, 0), straight)
            a = gate_s[i, :, cols].astype(jnp.float32)
            b = up_s[i, :, cols].astype(jnp.float32)
            s = 0.5 * jnp.tanh(0.5 * a) + 0.5
            swish = a * s
            product = swish * b
            scaled = upstream * b
            ggate_s[i, :, cols] = (scaled * (s + swish * (1.0 - s))).astype(jnp.bfloat16)
            gup_s[i, :, cols] = (upstream * swish).astype(jnp.bfloat16)
            here = swish * scaled
            here = here[:, :128] + here[:, 128:]
            if f == 0:
                sum_s[rows, :] = here
            else:
                sum_s[rows, :] += here
            hid_f[rows, :] = jnp.where(turn, pltpu.roll(product, UNIT - CAP, 0), product)
            for n, (src, dst) in enumerate(((ggate_s, grad_gate), (gup_s, grad_up))):
                copy = pltpu.make_async_copy(
                    src.at[i, :, cols],
                    dst.at[pl.ds(places[i], UNIT), cols],
                    sem_out.at[f, i, n],
                )
                copy.start()
                stores.append(copy)
        pieces, base = [], 0
        for size in sizes:
            for side in range(2):
                for j in range(size):
                    start = pl.multiple_of((base + j) * UNIT + sp[side], 8)
                    pieces.append(hid_f[pl.ds(start, PAIR), :])
                gap = padded(size * PAIR) - size * PAIR
                if gap:
                    pieces.append(jnp.zeros((gap, FT), jnp.float32))
            base += size
        hid[:, cols] = jnp.concatenate(pieces, axis=0).astype(jnp.bfloat16)
        copy = pltpu.make_async_copy(hid.at[:, cols], hid_out.at[wide, cols], sem_h.at[f])
        copy.start()
        stores.append(copy)
    ones = jnp.ones((8, 128), jnp.float32)
    for i in range(units):
        term_s[i] = lax.dot_general(
            ones,
            sum_s[pl.ds(i * UNIT, UNIT), :],
            NT,
            precision=lax.Precision.HIGHEST,
            preferred_element_type=jnp.float32,
        )
        copy = pltpu.make_async_copy(term_s.at[i], term.at[sp[5 + i]], sem_t.at[i])
        copy.start()
        stores.append(copy)
    for copy in stores:
        copy.wait()


def run_act(sizes, sp, ys, weights, gate, up, carried, offset=0, total=None):
    units = sum(sizes)
    vmem = pl.BlockSpec(memory_space=pltpu.VMEM)
    anywhere = pl.BlockSpec(memory_space=pltpu.HBM)
    first, last = carried is None, total is None
    in_specs = [pl.BlockSpec(memory_space=pltpu.SMEM)] + [vmem] * (len(ys) + 2) + [anywhere] * 2
    operands = [sp] + [held(y) for y in ys] + list(weights) + [gate, up]
    aliases = {}
    if not first:
        at = len(operands)
        in_specs += [anywhere] * len(carried)
        operands += list(carried)
        aliases = {at + n: n for n in range(len(carried))}
    bf16, f32 = jnp.bfloat16, jnp.float32
    tall = units * UNIT
    wide = sum(padded(y.shape[0]) for y in ys)
    out = pl.pallas_call(
        functools.partial(act_kernel, sizes, offset, first, last),
        in_specs=in_specs,
        out_specs=[anywhere] * (6 if last else 5),
        out_shape=[
            pltpu.HBM((ROWS, FF), bf16),
            pltpu.HBM((ROWS, FF), bf16),
            pltpu.HBM((16, 8, UNIT), f32),
            pltpu.HBM((wide if last else total, FF), bf16),
            pltpu.HBM((wide if last else total, D), bf16),
        ]
        + [pltpu.HBM((wide, HALF), bf16)] * last,
        scratch_shapes=[pltpu.VMEM((wide, D), bf16), pltpu.VMEM((wide, FF), bf16)]
        + [pltpu.VMEM((units, UNIT, FF), bf16)] * 4
        + [
            pltpu.VMEM((2, tall, FT), f32),
            pltpu.VMEM((2, tall, FT), f32),
            pltpu.VMEM((tall, 128), f32),
            pltpu.VMEM((units, 8, UNIT), f32),
            pltpu.SemaphoreType.DMA((units, 2)),
            pltpu.SemaphoreType.DMA((FF // FT, units, 2)),
            pltpu.SemaphoreType.DMA((units,)),
            pltpu.SemaphoreType.DMA((FF // FT,)),
            pltpu.SemaphoreType.DMA((2,)),
        ],
        input_output_aliases=aliases,
        cost_estimate=pl.CostEstimate(
            flops=200_000_000_000 if last else 1, bytes_accessed=1, transcendentals=0
        ),
        compiler_params=pltpu.CompilerParams(vmem_limit_bytes=38 * MIB),
    )(*operands)
    return out


def wgrad_kernel(pairs, sums_n, outs_n, *refs):
    hids, rows, refs = refs[:pairs], refs[pairs : 2 * pairs], refs[2 * pairs :]
    sums, outs = refs[:sums_n], refs[sums_n:]
    total = None
    for s in sums:
        part = s[...].astype(jnp.float32)
        total = part if total is None else total + part
    for hid, y in zip(hids, rows):
        part = lax.dot_general(hid[...], y[...], TN, preferred_element_type=jnp.float32)
        total = part if total is None else total + part
    if outs_n == 1:
        outs[0][...] = total.astype(outs[0].dtype)
    else:
        step = pl.program_id(0)

        @pl.when(step < HALF // NTILE)
        def _():
            outs[1][...] = total.astype(outs[1].dtype)

        @pl.when(step >= HALF // NTILE)
        def _():
            outs[0][...] = total.astype(outs[0].dtype)


def run_wgrad(hids, ys, sums, out_types):
    halves = len(out_types)
    steps = HALF // NTILE
    if halves == 2:
        cols = lambda n: lax.rem(n + steps, 2 * steps)
        specs = [
            pl.BlockSpec((FF, NTILE), lambda n: (0, jnp.maximum(n - steps, 0))),
            pl.BlockSpec((FF, NTILE), lambda n: (0, jnp.minimum(n, steps - 1))),
        ]
    else:
        cols = lambda n: n
        specs = [pl.BlockSpec((FF, NTILE), lambda n: (0, n))]
    return pl.pallas_call(
        functools.partial(wgrad_kernel, len(hids), len(sums), halves),
        grid=(halves * steps,),
        in_specs=[pl.BlockSpec(h.shape, lambda n: (0, 0)) for h in hids]
        + [pl.BlockSpec((y.shape[0], NTILE), lambda n: (0, cols(n))) for y in ys]
        + [pl.BlockSpec((FF, NTILE), lambda n: (0, n))] * len(sums),
        out_specs=specs,
        out_shape=[pltpu.HBM((FF, HALF), t) for t in out_types],
        cost_estimate=pl.CostEstimate(flops=1, bytes_accessed=1, transcendentals=0),
        compiler_params=pltpu.CompilerParams(vmem_limit_bytes=34 * MIB),
    )(*map(outside, hids), *map(outside, ys), *map(outside, sums))


def keep_kernel(source, out, sem):
    copy = pltpu.make_async_copy(source, out, sem)
    copy.start()
    copy.wait()


def keep(array):
    return pl.pallas_call(
        keep_kernel,
        in_specs=[pl.BlockSpec(memory_space=pltpu.HBM)],
        out_specs=pl.BlockSpec(memory_space=pltpu.VMEM),
        out_shape=jax.ShapeDtypeStruct(array.shape, array.dtype),
        scratch_shapes=[pltpu.SemaphoreType.DMA],
        cost_estimate=pl.CostEstimate(flops=1, bytes_accessed=1, transcendentals=0),
        compiler_params=pltpu.CompilerParams(vmem_limit_bytes=8 * MIB),
    )(outside(array))


def local(grad_out, expert_ids, gate_probs, keep_mask, pre_gate, pre_up, w_down):
    dp = lax.axis_index("dp")
    expert = lax.axis_index("expert")
    etp = lax.axis_index("etp")
    x_lo, z = expert // 4, expert % 4
    x_hi, y = etp // 4, etp % 4
    x = x_hi * 2 + x_lo
    turned_y = (y - dp) % 4
    pair = turned_y // 2

    par_x = move(grad_out, near_pair)
    own_w = w_down[0]
    oth_w = move(own_w, other_core)
    kept = gate_probs * keep_mask.astype(jnp.bfloat16)
    meta = jnp.concatenate(
        [
            expert_ids.T.astype(jnp.float32),
            kept.T.astype(jnp.float32),
            jnp.zeros((4, TOK), jnp.float32),
        ],
        axis=0,
    )
    par_meta = move(meta, near_pair)
    kept_w = keep(own_w)
    weights = held(kept_w), held(oth_w)

    sp = jnp.stack([z, x_lo, turned_y % 2]).astype(jnp.int32)
    s0, s1, s2, s3, slots = build_slots(sp, meta, par_meta, grad_out, after(par_x, oth_w, kept_w))

    def place(away_x, away_z):
        source_x, source_z = (x + away_x) % 4, (z + away_z) % 4
        return ((source_x % 2) * 4 + source_z) * 2 + source_x // 2

    common = [pair * PAIR, (1 - pair) * PAIR, dp, dp * HALF, (1 - dp) * HALF]

    def scalars(places):
        return jnp.stack(common + places).astype(jnp.int32)

    cat = lambda *parts: jnp.concatenate(parts, axis=0)
    gate, up = outside(pre_gate[0]), outside(pre_up[0])

    same0, other0 = s0[:PAIR], s0[PAIR:]
    z1 = move(s1, along_z(1))
    z3 = move(s3, along_z(-1))
    n0l = move(other0, along_x(1))
    n0r = move(other0, along_x(-1))
    o0 = move(same0, along_x(2))
    own0 = cat(same0, n0l, n0r)
    par0 = move(own0, far_pair)

    z1, z3, o0 = lax.optimization_barrier((z1, z3, o0))
    o13 = cat(z1[:PAIR], z3[:PAIR])
    n13 = cat(z1[PAIR:], z3[PAIR:])
    own1 = [o0, o13]
    par1 = [move(v, far_pair) for v in own1]
    n13l = move(n13, along_x(1))
    n13r = move(n13, along_x(-1))
    z2 = move(after(s2, z1, z3), along_z(2))

    n13l, n13r, z2, par0 = lax.optimization_barrier((n13l, n13r, z2, par0))
    own2 = [n13l, n13r]
    par2 = [move(v, far_pair) for v in own2]
    o13r = move(after(o13, n13l), along_x(2))
    same2, other2 = z2[:PAIR], z2[PAIR:]
    n2l = move(other2, along_x(1))
    n2r = move(other2, along_x(-1))

    sp_a = scalars(
        [place(0, 0), place(-1, 0), place(1, 0), place(2, 0), place(0, -1), place(0, 1)]
    )
    early = [own0, par0, own1[0], par1[0], own1[1], par1[1]]
    size_a = sum(padded(v.shape[0]) for v in early)
    size_b = 4 * 2 * PAIR
    filled = run_act((3, 1, 2), sp_a, early, weights, gate, up, None, 0, size_a + size_b)

    o13r, same2 = lax.optimization_barrier((o13r, same2, filled[3]))[:2]
    own3 = [o13r, same2]
    par3 = [move(v, far_pair) for v in own3]
    o2 = move(same2, along_x(2))
    sp_b = scalars([place(-1, -1), place(-1, 1), place(1, -1), place(1, 1)])
    middle = [own2[0], par2[0], own2[1], par2[1]]
    filled = run_act(
        (2, 2), sp_b, middle, weights, gate, up, filled, size_a, size_a + size_b
    )

    n2l, n2r = lax.optimization_barrier((n2l, n2r, filled[3]))[:2]
    own4 = [n2l, n2r]
    par4 = [move(v, far_pair) for v in own4]
    own_sum, oth_sum = run_wgrad(
        [filled[3]], [filled[4]], [], [jnp.float32, jnp.bfloat16]
    )
    far_sum = move(oth_sum, other_core)
    own5 = o2
    par5 = after(move(own5, far_pair), own_sum)

    sp_c = scalars(
        [place(2, -1), place(2, 1), place(0, 2), place(-1, 2), place(1, 2), place(2, 2)]
    )
    late = [own3[0], par3[0], own3[1], par3[1], own4[0], par4[0], own4[1], par4[1], own5, par5]
    grad_gate, grad_up, term, hid_c, rows_c, far_rows = run_act(
        (2, 1, 1, 1, 1), sp_c, late, weights, gate, up, filled[:3]
    )
    far_rows = move(far_rows, other_core)
    far_hid = move(hid_c, other_core)
    returned = lax.all_to_all(
        term[:, 0, :].reshape(64, CAP), ("expert", "etp"), split_axis=0, concat_axis=0, tiled=True
    )
    (grad_w,) = run_wgrad(
        [hid_c, far_hid], [rows_c, far_rows], [own_sum, far_sum], [jnp.bfloat16]
    )
    returned, grad_w = lax.optimization_barrier((returned, grad_w))

    summed = returned.reshape(EXPERTS, 8, CAP).sum(axis=1)
    hit = (expert_ids.T[:, :, None, None] == jnp.arange(EXPERTS)[None, None, :, None]) & (
        slots[:2, :, None, None] == jnp.arange(CAP, dtype=jnp.float32)[None, None, None, :]
    )
    picked = jnp.sum(jnp.where(hit, summed[None, None], 0.0), axis=(2, 3)).T
    kept_only = keep_mask.astype(jnp.float32) * picked
    grad_gate_probs = kept_only / gate_probs.astype(jnp.float32)
    return (grad_gate[None], grad_up[None], grad_w[None], grad_gate_probs)


def solution(mesh):
    tokens = P(("dp", "expert", "etp"), None)
    acts = P("expert", "dp", "etp")
    weight = P("expert", "etp", "dp")
    return jax.shard_map(
        local,
        mesh=mesh,
        in_specs=(tokens, tokens, tokens, tokens, acts, acts, weight),
        out_specs=(acts, acts, weight, tokens),
        check_vma=False,
    )
```

```python
import functools

import jax
import jax.numpy as jnp
from jax import lax
from jax.experimental import pallas as pl
from jax.experimental.pallas import tpu as pltpu
from jax.sharding import PartitionSpec as P

AXES = ("dp", "expert", "etp")
EXPERTS = 8
CAP = 36
TOK = 128
D = 3072
HALF = 1536
FF = 1024
ROWS = 2304
PAIR = 2 * CAP
UNIT = 4 * CAP
FT = 512
NTILE = 512
MIB = 1024 * 1024
NT = (((1,), (1,)), ((), ()))
TN = (((0,), (0,)), ((), ()))


def position(flat):
    dp, rest = divmod(flat, 64)
    expert, etp = divmod(rest, 8)
    x_lo, z = divmod(expert, 4)
    x_hi, y = divmod(etp, 4)
    return dp, x_hi * 2 + x_lo, y, z


def flat_of(dp, x, y, z):
    return dp * 64 + ((x % 2) * 4 + z) * 8 + (x // 2) * 4 + y


def move(array, step):
    pairs = []
    for source in range(128):
        dp, x, y, z = position(source)
        pairs.append((source, flat_of(*step(dp, x, y, z))))
    return lax.ppermute(array, AXES, pairs)


def along_x(k):
    return lambda dp, x, y, z: (dp, (x + k) % 4, y, z)


def along_z(k):
    return lambda dp, x, y, z: (dp, x, y, (z + k) % 4)


def turned(dp, y, change):
    return (change((y - dp) % 4) + dp) % 4


def near_pair(dp, x, y, z):
    return dp, x, turned(dp, y, lambda v: v ^ 1), z


def far_pair(dp, x, y, z):
    return dp, x, turned(dp, y, lambda v: 3 - v), z


def other_core(dp, x, y, z):
    return 1 - dp, x, y, z


def after(value, *others):
    return lax.optimization_barrier((value,) + others)[0]


def held(array):
    return pltpu.with_memory_space_constraint(array, pltpu.VMEM)


def outside(array):
    return pltpu.with_memory_space_constraint(array, pltpu.HBM)


def slot_lines(meta):
    names = lax.broadcasted_iota(jnp.int32, (EXPERTS, TOK), 0).astype(jnp.float32)
    first = (names == meta[0:1, :]).astype(jnp.float32)
    second = (names == meta[1:2, :]).astype(jnp.float32)
    row = lax.broadcasted_iota(jnp.int32, (TOK, TOK), 0)
    col = lax.broadcasted_iota(jnp.int32, (TOK, TOK), 1)
    earlier = (row < col).astype(jnp.bfloat16)
    before = jnp.dot(
        (first + second).astype(jnp.bfloat16), earlier, preferred_element_type=jnp.float32
    )
    return (
        jnp.sum(before * first, axis=0, keepdims=True),
        jnp.sum(before * second, axis=0, keepdims=True),
    )


def slots_kernel(sp, own_meta, par_meta, own_x, par_x, *refs):
    outs, both = refs[:-1], refs[-1]
    both[:TOK, :] = own_x[...]
    both[TOK:, :] = par_x[...]
    z, x_lo, odd = sp[0], sp[1], sp[2]
    own_slots = slot_lines(own_meta[...])
    par_slots = slot_lines(par_meta[...])
    outs[-1][...] = jnp.concatenate(
        [own_slots[0], own_slots[1], jnp.zeros((6, TOK), jnp.float32)], axis=0
    )
    row = lax.broadcasted_iota(jnp.int32, (UNIT, 1), 0)
    other = row >= PAIR
    within = jnp.where(other, row - PAIR, row)
    late = (within >= CAP).astype(jnp.int32)
    slot = jnp.where(within >= CAP, within - CAP, within).astype(jnp.float32)
    lo = jnp.where(other, 1 - x_lo, x_lo)
    picks = []
    for mine, meta, slots in ((True, own_meta, own_slots), (False, par_meta, par_slots)):
        here = late == (odd if mine else 1 - odd)
        rows = []
        for k in range(4):
            expert = (lo * 4 + lax.rem(z + k, 4)).astype(jnp.float32)
            pick = jnp.zeros((UNIT, TOK), jnp.float32)
            for j in range(2):
                hit = (meta[j : j + 1, :] == expert) & (slots[j] == slot) & here
                pick = pick + jnp.where(hit, meta[2 + j : 3 + j, :], 0.0)
            rows.append(pick)
        picks.append(jnp.concatenate(rows, axis=0).astype(jnp.bfloat16))
    pick = jnp.concatenate(picks, axis=1)
    step = 512
    for at in range(0, D, step):
        cols = slice(at, at + step)
        total = jnp.dot(pick, both[:, cols], preferred_element_type=jnp.float32)
        total = total.astype(jnp.bfloat16)
        at = 0
        for out in outs[:-1]:
            out[:, cols] = total[at : at + out.shape[0]]
            at += out.shape[0]


def build_slots(sp, own_meta, par_meta, own_x, par_x):
    vmem = pl.BlockSpec(memory_space=pltpu.VMEM)
    return pl.pallas_call(
        slots_kernel,
        in_specs=[pl.BlockSpec(memory_space=pltpu.SMEM)] + [vmem] * 4,
        out_specs=[vmem] * 6,
        out_shape=[
            jax.ShapeDtypeStruct((rows, D), jnp.bfloat16)
            for rows in (PAIR, PAIR, UNIT, UNIT, UNIT)
        ]
        + [jax.ShapeDtypeStruct((8, TOK), jnp.float32)],
        scratch_shapes=[pltpu.VMEM((2 * TOK, D), jnp.bfloat16)],
        cost_estimate=pl.CostEstimate(flops=1, bytes_accessed=1, transcendentals=0),
        compiler_params=pltpu.CompilerParams(vmem_limit_bytes=16 * MIB),
    )(sp, own_meta, par_meta, held(own_x), held(par_x))


def padded(rows):
    return (rows + 15) // 16 * 16


def act_kernel(sizes, offset, first, last, sp, *refs):
    units = sum(sizes)
    ys, refs = refs[: 2 * len(sizes)], refs[2 * len(sizes) :]
    w_halves, gate, up, refs = refs[:2], refs[2], refs[3], refs[4:]
    if not first:
        refs = refs[3 if last else 4 :]
    grad_gate, grad_up, term, hid_out = refs[:4]
    far_out, refs = (refs[4], refs[5:]) if last else (None, refs[4:])
    rows_s, hid, gate_s, up_s, ggate_s, gup_s, back_s, hid_s, sum_s, term_s = refs[:10]
    sem_in, sem_out, sem_t, sem_h, sem_r = refs[10:]
    places = [pl.multiple_of(sp[5 + i] * UNIT, UNIT) for i in range(units)]
    loads = []
    for i in range(units):
        rows = pl.ds(places[i], UNIT)
        loads.append(
            (
                pltpu.make_async_copy(gate.at[rows, :], gate_s.at[i], sem_in.at[i, 0]),
                pltpu.make_async_copy(up.at[rows, :], up_s.at[i], sem_in.at[i, 1]),
            )
        )
    for pair in loads:
        for copy in pair:
            copy.start()
    starts, at = [], 0
    for n, y in enumerate(ys):
        rows = y.shape[0]
        starts.append(at)
        for h in range(2):
            cols = pl.ds(pl.multiple_of(sp[3 + h], 128), HALF)
            rows_s[at : at + rows, h * HALF : (h + 1) * HALF] = y[:, cols]
        gap = padded(rows) - rows
        if gap:
            rows_s[at + rows : at + rows + gap, :] = jnp.zeros((gap, D), jnp.bfloat16)
        at += rows + gap
    turn = sp[2] > 0
    wide = pl.ds(offset, rows_s.shape[0])
    stores = []
    if last:
        copy = pltpu.make_async_copy(rows_s.at[:, pl.ds(HALF, HALF)], far_out, sem_r.at[0])
        copy.start()
        stores.append(copy)

    def back_of(f):
        cols = pl.ds(f * FT, FT)
        return lax.dot_general(
            rows_s[:, :HALF], w_halves[0][cols, :], NT, preferred_element_type=jnp.float32
        ) + lax.dot_general(
            rows_s[:, HALF:], w_halves[1][cols, :], NT, preferred_element_type=jnp.float32
        )

    later = back_of(0)
    for f in range(FF // FT):
        cols = pl.ds(f * FT, FT)
        back_f, hid_f = back_s.at[f % 2], hid_s.at[f % 2]
        back = later
        base = 0
        for g, size in enumerate(sizes):
            for side in range(2):
                for j in range(size):
                    start = pl.multiple_of((base + j) * UNIT + sp[side], 8)
                    piece = starts[2 * g + side] + j * PAIR
                    back_f[pl.ds(start, PAIR), :] = back[piece : piece + PAIR]
            base += size
        if f + 1 < FF // FT:
            later = back_of(f + 1)
        for i in range(units):
            rows = pl.ds(i * UNIT, UNIT)
            if f == 0:
                for copy in loads[i]:
                    copy.wait()
            straight = back_f[rows, :]
            upstream = jnp.where(turn, pltpu.roll(straight, CAP, 0), straight)
            a = gate_s[i, :, cols].astype(jnp.float32)
            b = up_s[i, :, cols].astype(jnp.float32)
            s = 0.5 * jnp.tanh(0.5 * a) + 0.5
            swish = a * s
            product = swish * b
            scaled = upstream * b
            ggate_s[i, :, cols] = (scaled * (s + swish * (1.0 - s))).astype(jnp.bfloat16)
            gup_s[i, :, cols] = (upstream * swish).astype(jnp.bfloat16)
            here = swish * scaled
            here = here[:, :128] + here[:, 128:256] + here[:, 256:384] + here[:, 384:]
            if f == 0:
                sum_s[rows, :] = here
            else:
                sum_s[rows, :] += here
            hid_f[rows, :] = jnp.where(turn, pltpu.roll(product, UNIT - CAP, 0), product)
            for n, (src, dst) in enumerate(((ggate_s, grad_gate), (gup_s, grad_up))):
                copy = pltpu.make_async_copy(
                    src.at[i, :, cols],
                    dst.at[pl.ds(places[i], UNIT), cols],
                    sem_out.at[f, i, n],
                )
                copy.start()
                stores.append(copy)
        pieces, base = [], 0
        for size in sizes:
            for side in range(2):
                for j in range(size):
                    start = pl.multiple_of((base + j) * UNIT + sp[side], 8)
                    pieces.append(hid_f[pl.ds(start, PAIR), :])
                gap = padded(size * PAIR) - size * PAIR
                if gap:
                    pieces.append(jnp.zeros((gap, FT), jnp.float32))
            base += size
        hid[:, cols] = jnp.concatenate(pieces, axis=0).astype(jnp.bfloat16)
        copy = pltpu.make_async_copy(hid.at[:, cols], hid_out.at[wide, cols], sem_h.at[f])
        copy.start()
        stores.append(copy)
    ones = jnp.ones((8, 128), jnp.float32)
    for i in range(units):
        term_s[i] = lax.dot_general(
            ones,
            sum_s[pl.ds(i * UNIT, UNIT), :],
            NT,
            precision=lax.Precision.HIGHEST,
            preferred_element_type=jnp.float32,
        )
        copy = pltpu.make_async_copy(term_s.at[i], term.at[sp[5 + i]], sem_t.at[i])
        copy.start()
        stores.append(copy)
    for copy in stores:
        copy.wait()


def run_act(sizes, sp, ys, weights, gate, up, carried, offset=0, total=None):
    units = sum(sizes)
    vmem = pl.BlockSpec(memory_space=pltpu.VMEM)
    anywhere = pl.BlockSpec(memory_space=pltpu.HBM)
    first, last = carried is None, total is None
    in_specs = [pl.BlockSpec(memory_space=pltpu.SMEM)] + [vmem] * (len(ys) + 2) + [anywhere] * 2
    operands = [sp] + [held(y) for y in ys] + list(weights) + [gate, up]
    aliases = {}
    if not first:
        at = len(operands)
        in_specs += [anywhere] * len(carried)
        operands += list(carried)
        aliases = {at + n: n for n in range(len(carried))}
    bf16, f32 = jnp.bfloat16, jnp.float32
    tall = units * UNIT
    wide = sum(padded(y.shape[0]) for y in ys)
    out = pl.pallas_call(
        functools.partial(act_kernel, sizes, offset, first, last),
        in_specs=in_specs,
        out_specs=[anywhere] * (5 if last else 4),
        out_shape=[
            pltpu.HBM((ROWS, FF), bf16),
            pltpu.HBM((ROWS, FF), bf16),
            pltpu.HBM((16, 8, UNIT), f32),
            pltpu.HBM((wide if last else total, FF), bf16),
        ]
        + [pltpu.HBM((wide, HALF), bf16)] * last,
        scratch_shapes=[pltpu.VMEM((wide, D), bf16), pltpu.VMEM((wide, FF), bf16)]
        + [pltpu.VMEM((units, UNIT, FF), bf16)] * 4
        + [
            pltpu.VMEM((2, tall, FT), f32),
            pltpu.VMEM((2, tall, FT), f32),
            pltpu.VMEM((tall, 128), f32),
            pltpu.VMEM((units, 8, UNIT), f32),
            pltpu.SemaphoreType.DMA((units, 2)),
            pltpu.SemaphoreType.DMA((FF // FT, units, 2)),
            pltpu.SemaphoreType.DMA((units,)),
            pltpu.SemaphoreType.DMA((FF // FT,)),
            pltpu.SemaphoreType.DMA((1,)),
        ],
        input_output_aliases=aliases,
        cost_estimate=pl.CostEstimate(
            flops=200_000_000_000 if last else 1, bytes_accessed=1, transcendentals=0
        ),
        compiler_params=pltpu.CompilerParams(vmem_limit_bytes=(38 if units > 4 else 5 * units + 4) * MIB),
    )(*operands)
    return out


def wgrad_kernel(count, far, sums_n, outs_n, sp, hid, *refs):
    ys, refs = refs[:count], refs[count:]
    if far:
        (far_hid, far_rows), refs = refs[:2], refs[2:]
    sums, outs, rows = refs[:sums_n], refs[sums_n:-1], refs[-1]
    step, steps = pl.program_id(0), HALF // NTILE
    cols = sp[3] + step * NTILE
    if outs_n == 2:
        cols = jnp.where(step < steps, sp[4] + step * NTILE, sp[3] + (step - steps) * NTILE)
    cols = pl.ds(pl.multiple_of(cols, 128), NTILE)
    at = 0
    for y in ys:
        size = y.shape[0]
        rows[at : at + size, :] = y[:, cols]
        gap = padded(size) - size
        if gap:
            rows[at + size : at + size + gap, :] = jnp.zeros((gap, NTILE), jnp.bfloat16)
        at += size + gap
    total = lax.dot_general(hid[...], rows[...], TN, preferred_element_type=jnp.float32)
    if far:
        here = pl.ds(pl.multiple_of(step * NTILE, 128), NTILE)
        total += lax.dot_general(
            far_hid[...], far_rows[:, here], TN, preferred_element_type=jnp.float32
        )
    for s in sums:
        total += s[...].astype(jnp.float32)
    if outs_n == 1:
        outs[0][...] = total.astype(outs[0].dtype)
    else:

        @pl.when(step < steps)
        def _():
            outs[1][...] = total.astype(outs[1].dtype)

        @pl.when(step >= steps)
        def _():
            outs[0][...] = total.astype(outs[0].dtype)


def run_wgrad(sp, hid, ys, far, sums, out_types):
    vmem = pl.BlockSpec(memory_space=pltpu.VMEM)
    halves = len(out_types)
    steps = HALF // NTILE
    tile = pl.BlockSpec((FF, NTILE), lambda n: (0, n))
    specs = [tile]
    if halves == 2:
        specs = [
            pl.BlockSpec((FF, NTILE), lambda n: (0, jnp.maximum(n - steps, 0))),
            pl.BlockSpec((FF, NTILE), lambda n: (0, jnp.minimum(n, steps - 1))),
        ]
    whole = lambda a: pl.BlockSpec(a.shape, lambda n: (0, 0))
    return pl.pallas_call(
        functools.partial(wgrad_kernel, len(ys), len(far) > 0, len(sums), halves),
        grid=(halves * steps,),
        in_specs=[pl.BlockSpec(memory_space=pltpu.SMEM), vmem if far else whole(hid)]
        + [vmem] * (len(ys) + len(far))
        + [tile] * len(sums),
        out_specs=specs,
        out_shape=[pltpu.HBM((FF, HALF), t) for t in out_types],
        scratch_shapes=[pltpu.VMEM((hid.shape[0], NTILE), jnp.bfloat16)],
        cost_estimate=pl.CostEstimate(flops=1, bytes_accessed=1, transcendentals=0),
        compiler_params=pltpu.CompilerParams(vmem_limit_bytes=24 * MIB),
    )(sp, held(hid) if far else outside(hid), *map(held, ys), *map(held, far), *map(outside, sums))


def keep_kernel(source, out, sem):
    copy = pltpu.make_async_copy(source, out, sem)
    copy.start()
    copy.wait()


def keep(array):
    return pl.pallas_call(
        keep_kernel,
        in_specs=[pl.BlockSpec(memory_space=pltpu.HBM)],
        out_specs=pl.BlockSpec(memory_space=pltpu.VMEM),
        out_shape=jax.ShapeDtypeStruct(array.shape, array.dtype),
        scratch_shapes=[pltpu.SemaphoreType.DMA],
        cost_estimate=pl.CostEstimate(flops=1, bytes_accessed=1, transcendentals=0),
        compiler_params=pltpu.CompilerParams(vmem_limit_bytes=8 * MIB),
    )(outside(array))


def local(grad_out, expert_ids, gate_probs, keep_mask, pre_gate, pre_up, w_down):
    dp = lax.axis_index("dp")
    expert = lax.axis_index("expert")
    etp = lax.axis_index("etp")
    x_lo, z = expert // 4, expert % 4
    x_hi, y = etp // 4, etp % 4
    x = x_hi * 2 + x_lo
    turned_y = (y - dp) % 4
    pair = turned_y // 2

    par_x = move(grad_out, near_pair)
    own_w = w_down[0]
    oth_w = move(own_w, other_core)
    kept = gate_probs * keep_mask.astype(jnp.bfloat16)
    meta = jnp.concatenate(
        [
            expert_ids.T.astype(jnp.float32),
            kept.T.astype(jnp.float32),
            jnp.zeros((4, TOK), jnp.float32),
        ],
        axis=0,
    )
    par_meta = move(meta, near_pair)
    kept_w = keep(own_w)
    weights = held(kept_w), held(oth_w)

    sp = jnp.stack([z, x_lo, turned_y % 2]).astype(jnp.int32)
    same0, other0, s1, s2, s3, slots = build_slots(sp, meta, par_meta, grad_out, after(par_x, oth_w, kept_w))

    def place(away_x, away_z):
        source_x, source_z = (x + away_x) % 4, (z + away_z) % 4
        return ((source_x % 2) * 4 + source_z) * 2 + source_x // 2

    common = [pair * PAIR, (1 - pair) * PAIR, dp, dp * HALF, (1 - dp) * HALF]

    def scalars(places):
        return jnp.stack(common + places).astype(jnp.int32)

    cat = lambda *parts: jnp.concatenate(parts, axis=0)
    gate, up = outside(pre_gate[0]), outside(pre_up[0])

    z1 = move(s1, along_z(1))
    z3 = move(s3, along_z(-1))
    n0l = move(other0, along_x(1))
    n0r = move(other0, along_x(-1))
    o0 = move(after(same0, n0l, n0r), along_x(2))
    own0 = cat(same0, n0l, n0r)
    par0 = move(own0, far_pair)

    z1, z3, o0 = lax.optimization_barrier((z1, z3, o0))
    o13 = cat(z1[:PAIR], z3[:PAIR])
    n13 = cat(z1[PAIR:], z3[PAIR:])
    own1 = [o0, o13]
    par1 = [move(v, far_pair) for v in own1]
    n13l = move(n13, along_x(1))
    n13r = move(n13, along_x(-1))
    z2 = move(after(s2, z1, z3), along_z(2))

    size_a, size_b, size_c = 2 * padded(3 * PAIR), 2 * (padded(PAIR) + 2 * PAIR), 8 * PAIR
    total = size_a + size_b + size_c
    sp_a = scalars([place(0, 0), place(-1, 0), place(1, 0)])
    rows_a = [own0, par0]
    filled = run_act((3,), sp_a, rows_a, weights, gate, up, None, 0, total)

    n13l, n13r, z2, par1[0] = lax.optimization_barrier(
        (n13l, n13r, z2, par1[0], filled[3])
    )[:4]
    same2, other2 = z2[:PAIR], z2[PAIR:]
    own2 = [n13l, n13r]
    par2 = [move(v, far_pair) for v in own2]
    o13r = move(after(o13, n13l), along_x(2))
    n2l = move(other2, along_x(1))
    n2r = move(other2, along_x(-1))

    sp_b = scalars([place(2, 0), place(0, -1), place(0, 1)])
    rows_b = [own1[0], par1[0], own1[1], par1[1]]
    filled = run_act((1, 2), sp_b, rows_b, weights, gate, up, filled, size_a, total)

    o13r, same2 = lax.optimization_barrier((o13r, same2, filled[3]))[:2]
    own3 = [o13r, same2]
    par3 = [move(v, far_pair) for v in own3]
    o2 = move(same2, along_x(2))
    sp_c = scalars([place(-1, -1), place(-1, 1), place(1, -1), place(1, 1)])
    rows_c = [own2[0], par2[0], own2[1], par2[1]]
    filled = run_act((2, 2), sp_c, rows_c, weights, gate, up, filled, size_a + size_b, total)

    n2l, n2r, par3[1] = lax.optimization_barrier((n2l, n2r, par3[1], filled[3]))[:3]
    own4 = [n2l, n2r]
    par4 = [move(v, far_pair) for v in own4]
    own_sum, oth_sum = run_wgrad(
        sp_c, filled[3], rows_a + rows_b + rows_c, [], [], [jnp.bfloat16, jnp.bfloat16]
    )
    far_sum = move(oth_sum, other_core)
    own5 = o2
    par5 = after(move(own5, far_pair), own_sum)

    sp_d = scalars(
        [place(2, -1), place(2, 1), place(0, 2), place(-1, 2), place(1, 2), place(2, 2)]
    )
    late = [own3[0], par3[0], own3[1], par3[1], own4[0], par4[0], own4[1], par4[1], own5, par5]
    grad_gate, grad_up, term, hid_d, far_rows = run_act(
        (2, 1, 1, 1, 1), sp_d, late, weights, gate, up, filled[:3]
    )
    far_rows = move(far_rows, other_core)
    far_hid = move(hid_d, other_core)
    returned = lax.all_to_all(
        term[:, 0, :].reshape(64, CAP), ("expert", "etp"), split_axis=0, concat_axis=0, tiled=True
    )
    (grad_w,) = run_wgrad(
        sp_d, hid_d, late, [far_hid, far_rows], [own_sum, far_sum], [jnp.bfloat16]
    )
    returned, grad_w = lax.optimization_barrier((returned, grad_w))

    summed = returned.reshape(EXPERTS, 8, CAP).sum(axis=1)
    hit = (expert_ids.T[:, :, None, None] == jnp.arange(EXPERTS)[None, None, :, None]) & (
        slots[:2, :, None, None] == jnp.arange(CAP, dtype=jnp.float32)[None, None, None, :]
    )
    picked = jnp.sum(jnp.where(hit, summed[None, None], 0.0), axis=(2, 3)).T
    kept_only = keep_mask.astype(jnp.float32) * picked
    grad_gate_probs = kept_only / gate_probs.astype(jnp.float32)
    return (grad_gate[None], grad_up[None], grad_w[None], grad_gate_probs)


def solution(mesh):
    tokens = P(("dp", "expert", "etp"), None)
    acts = P("expert", "dp", "etp")
    weight = P("expert", "etp", "dp")
    return jax.shard_map(
        local,
        mesh=mesh,
        in_specs=(tokens, tokens, tokens, tokens, acts, acts, weight),
        out_specs=(acts, acts, weight, tokens),
        check_vma=False,
    )
```

```python
import functools

import jax
import jax.numpy as jnp
from jax import lax
from jax.experimental import pallas as pl
from jax.experimental.pallas import tpu as pltpu
from jax.sharding import PartitionSpec as P

AXES = ("dp", "expert", "etp")
EXPERTS = 8
CAP = 36
TOK = 128
D = 3072
HALF = 1536
FF = 1024
ROWS = 2304
PAIR = 2 * CAP
UNIT = 4 * CAP
FT = 1024
NTILE = 512
MIB = 1024 * 1024
NT = (((1,), (1,)), ((), ()))
TN = (((0,), (0,)), ((), ()))


def position(flat):
    dp, rest = divmod(flat, 64)
    expert, etp = divmod(rest, 8)
    x_lo, z = divmod(expert, 4)
    x_hi, y = divmod(etp, 4)
    return dp, x_hi * 2 + x_lo, y, z


def flat_of(dp, x, y, z):
    return dp * 64 + ((x % 2) * 4 + z) * 8 + (x // 2) * 4 + y


def move(array, step):
    pairs = []
    for source in range(128):
        dp, x, y, z = position(source)
        pairs.append((source, flat_of(*step(dp, x, y, z))))
    return lax.ppermute(array, AXES, pairs)


def along_x(k):
    return lambda dp, x, y, z: (dp, (x + k) % 4, y, z)


def along_z(k):
    return lambda dp, x, y, z: (dp, x, y, (z + k) % 4)


def turned(dp, y, change):
    return (change((y - dp) % 4) + dp) % 4


def near_pair(dp, x, y, z):
    return dp, x, turned(dp, y, lambda v: v ^ 1), z


def far_pair(dp, x, y, z):
    return dp, x, turned(dp, y, lambda v: 3 - v), z


def other_core(dp, x, y, z):
    return 1 - dp, x, y, z


def after(value, *others):
    return lax.optimization_barrier((value,) + others)[0]


def held(array):
    return pltpu.with_memory_space_constraint(array, pltpu.VMEM)


def outside(array):
    return pltpu.with_memory_space_constraint(array, pltpu.HBM)


def slot_lines(meta):
    names = lax.broadcasted_iota(jnp.int32, (EXPERTS, TOK), 0).astype(jnp.float32)
    first = (names == meta[0:1, :]).astype(jnp.float32)
    second = (names == meta[1:2, :]).astype(jnp.float32)
    row = lax.broadcasted_iota(jnp.int32, (TOK, TOK), 0)
    col = lax.broadcasted_iota(jnp.int32, (TOK, TOK), 1)
    earlier = (row < col).astype(jnp.bfloat16)
    before = jnp.dot(
        (first + second).astype(jnp.bfloat16), earlier, preferred_element_type=jnp.float32
    )
    return (
        jnp.sum(before * first, axis=0, keepdims=True),
        jnp.sum(before * second, axis=0, keepdims=True),
    )


def slots_kernel(sp, own_meta, par_meta, own_x, par_x, *refs):
    outs, both = refs[:-1], refs[-1]
    both[:TOK, :] = own_x[...]
    both[TOK:, :] = par_x[...]
    z, x_lo, odd = sp[0], sp[1], sp[2]
    own_slots = slot_lines(own_meta[...])
    par_slots = slot_lines(par_meta[...])
    outs[-1][...] = jnp.concatenate(
        [own_slots[0], own_slots[1], jnp.zeros((6, TOK), jnp.float32)], axis=0
    )
    row = lax.broadcasted_iota(jnp.int32, (UNIT, 1), 0)
    other = row >= PAIR
    within = jnp.where(other, row - PAIR, row)
    late = (within >= CAP).astype(jnp.int32)
    slot = jnp.where(within >= CAP, within - CAP, within).astype(jnp.float32)
    lo = jnp.where(other, 1 - x_lo, x_lo)
    picks = []
    for mine, meta, slots in ((True, own_meta, own_slots), (False, par_meta, par_slots)):
        here = late == (odd if mine else 1 - odd)
        rows = []
        for k in range(4):
            expert = (lo * 4 + lax.rem(z + k, 4)).astype(jnp.float32)
            pick = jnp.zeros((UNIT, TOK), jnp.float32)
            for j in range(2):
                hit = (meta[j : j + 1, :] == expert) & (slots[j] == slot) & here
                pick = pick + jnp.where(hit, meta[2 + j : 3 + j, :], 0.0)
            rows.append(pick)
        picks.append(jnp.concatenate(rows, axis=0).astype(jnp.bfloat16))
    pick = jnp.concatenate(picks, axis=1)
    step = 512
    for at in range(0, D, step):
        cols = slice(at, at + step)
        total = jnp.dot(pick, both[:, cols], preferred_element_type=jnp.float32)
        total = total.astype(jnp.bfloat16)
        at = 0
        for out in outs[:-1]:
            out[:, cols] = total[at : at + out.shape[0]]
            at += out.shape[0]


def build_slots(sp, own_meta, par_meta, own_x, par_x):
    vmem = pl.BlockSpec(memory_space=pltpu.VMEM)
    return pl.pallas_call(
        slots_kernel,
        in_specs=[pl.BlockSpec(memory_space=pltpu.SMEM)] + [vmem] * 4,
        out_specs=[vmem] * 6,
        out_shape=[
            jax.ShapeDtypeStruct((rows, D), jnp.bfloat16)
            for rows in (PAIR, PAIR, UNIT, UNIT, UNIT)
        ]
        + [jax.ShapeDtypeStruct((8, TOK), jnp.float32)],
        scratch_shapes=[pltpu.VMEM((2 * TOK, D), jnp.bfloat16)],
        cost_estimate=pl.CostEstimate(flops=1, bytes_accessed=1, transcendentals=0),
        compiler_params=pltpu.CompilerParams(vmem_limit_bytes=16 * MIB),
    )(sp, own_meta, par_meta, held(own_x), held(par_x))


def padded(rows):
    return (rows + 15) // 16 * 16


def act_kernel(sizes, offset, first, last, sp, *refs):
    units = sum(sizes)
    ys, refs = refs[: 2 * len(sizes)], refs[2 * len(sizes) :]
    w_halves, gate, up, refs = refs[:2], refs[2], refs[3], refs[4:]
    if not first:
        refs = refs[3 if last else 5 :]
    grad_gate, grad_up, term, hid_out = refs[:4]
    rows_outs, refs = (refs[4:6], refs[6:]) if last else (refs[4:5], refs[5:])
    rows_s, hid, gate_s, up_s, ggate_s, gup_s, back_s, hid_s, sum_s, term_s = refs[:10]
    sem_in, sem_out, sem_t, sem_h, sem_r = refs[10:]
    places = [pl.multiple_of(sp[5 + i] * UNIT, UNIT) for i in range(units)]
    loads = []
    for i in range(units):
        rows = pl.ds(places[i], UNIT)
        loads.append(
            (
                pltpu.make_async_copy(gate.at[rows, :], gate_s.at[i], sem_in.at[i, 0]),
                pltpu.make_async_copy(up.at[rows, :], up_s.at[i], sem_in.at[i, 1]),
            )
        )
    for pair in loads:
        for copy in pair:
            copy.start()
    starts, at = [], 0
    for n, y in enumerate(ys):
        rows = y.shape[0]
        starts.append(at)
        for h in range(2):
            cols = pl.ds(pl.multiple_of(sp[3 + h], 128), HALF)
            rows_s[at : at + rows, h * HALF : (h + 1) * HALF] = y[:, cols]
        gap = padded(rows) - rows
        if gap:
            rows_s[at + rows : at + rows + gap, :] = jnp.zeros((gap, D), jnp.bfloat16)
        at += rows + gap
    turn = sp[2] > 0
    wide = pl.ds(offset, rows_s.shape[0])
    if last:
        stores = [
            pltpu.make_async_copy(rows_s.at[:, pl.ds(n * HALF, HALF)], out, sem_r.at[n])
            for n, out in enumerate(rows_outs)
        ]
    else:
        stores = [pltpu.make_async_copy(rows_s, rows_outs[0].at[wide, :], sem_r.at[0])]
    for copy in stores:
        copy.start()

    def back_of(f):
        cols = pl.ds(f * FT, FT)
        return lax.dot_general(
            rows_s[:, :HALF], w_halves[0][cols, :], NT, preferred_element_type=jnp.float32
        ) + lax.dot_general(
            rows_s[:, HALF:], w_halves[1][cols, :], NT, preferred_element_type=jnp.float32
        )

    later = back_of(0)
    for f in range(FF // FT):
        cols = pl.ds(f * FT, FT)
        back_f, hid_f = back_s.at[f % back_s.shape[0]], hid_s.at[f % hid_s.shape[0]]
        back = later
        base = 0
        for g, size in enumerate(sizes):
            for side in range(2):
                for j in range(size):
                    start = pl.multiple_of((base + j) * UNIT + sp[side], 8)
                    piece = starts[2 * g + side] + j * PAIR
                    back_f[pl.ds(start, PAIR), :] = back[piece : piece + PAIR]
            base += size
        if f + 1 < FF // FT:
            later = back_of(f + 1)
        for i in range(units):
            rows = pl.ds(i * UNIT, UNIT)
            if f == 0:
                for copy in loads[i]:
                    copy.wait()
            straight = back_f[rows, :]
            upstream = jnp.where(turn, pltpu.roll(straight, CAP, 0), straight)
            a = gate_s[i, :, cols].astype(jnp.float32)
            b = up_s[i, :, cols].astype(jnp.float32)
            s = 0.5 * jnp.tanh(0.5 * a) + 0.5
            swish = a * s
            product = swish * b
            scaled = upstream * b
            ggate_s[i, :, cols] = (scaled * (s + swish * (1.0 - s))).astype(jnp.bfloat16)
            gup_s[i, :, cols] = (upstream * swish).astype(jnp.bfloat16)
            here = swish * scaled
            here = sum(here[:, c : c + 128] for c in range(0, FT, 128))
            if f == 0:
                sum_s[rows, :] = here
            else:
                sum_s[rows, :] += here
            hid_f[rows, :] = jnp.where(turn, pltpu.roll(product, UNIT - CAP, 0), product)
            for n, (src, dst) in enumerate(((ggate_s, grad_gate), (gup_s, grad_up))):
                copy = pltpu.make_async_copy(
                    src.at[i, :, cols],
                    dst.at[pl.ds(places[i], UNIT), cols],
                    sem_out.at[f, i, n],
                )
                copy.start()
                stores.append(copy)
        pieces, base = [], 0
        for size in sizes:
            for side in range(2):
                for j in range(size):
                    start = pl.multiple_of((base + j) * UNIT + sp[side], 8)
                    pieces.append(hid_f[pl.ds(start, PAIR), :])
                gap = padded(size * PAIR) - size * PAIR
                if gap:
                    pieces.append(jnp.zeros((gap, FT), jnp.float32))
            base += size
        hid[:, cols] = jnp.concatenate(pieces, axis=0).astype(jnp.bfloat16)
        copy = pltpu.make_async_copy(hid.at[:, cols], hid_out.at[wide, cols], sem_h.at[f])
        copy.start()
        stores.append(copy)
    ones = jnp.ones((8, 128), jnp.float32)
    for i in range(units):
        term_s[i] = lax.dot_general(
            ones,
            sum_s[pl.ds(i * UNIT, UNIT), :],
            NT,
            precision=lax.Precision.HIGHEST,
            preferred_element_type=jnp.float32,
        )
        copy = pltpu.make_async_copy(term_s.at[i], term.at[sp[5 + i]], sem_t.at[i])
        copy.start()
        stores.append(copy)
    for copy in stores:
        copy.wait()


def run_act(sizes, sp, ys, weights, gate, up, carried, offset=0, total=None):
    units = sum(sizes)
    vmem = pl.BlockSpec(memory_space=pltpu.VMEM)
    anywhere = pl.BlockSpec(memory_space=pltpu.HBM)
    first, last = carried is None, total is None
    in_specs = [pl.BlockSpec(memory_space=pltpu.SMEM)] + [vmem] * (len(ys) + 2) + [anywhere] * 2
    operands = [sp] + [held(y) for y in ys] + list(weights) + [gate, up]
    aliases = {}
    if not first:
        at = len(operands)
        in_specs += [anywhere] * len(carried)
        operands += list(carried)
        aliases = {at + n: n for n in range(len(carried))}
    bf16, f32 = jnp.bfloat16, jnp.float32
    tall = units * UNIT
    wide = sum(padded(y.shape[0]) for y in ys)
    out = pl.pallas_call(
        functools.partial(act_kernel, sizes, offset, first, last),
        in_specs=in_specs,
        out_specs=[anywhere] * (6 if last else 5),
        out_shape=[
            pltpu.HBM((ROWS, FF), bf16),
            pltpu.HBM((ROWS, FF), bf16),
            pltpu.HBM((16, 8, UNIT), f32),
            pltpu.HBM((wide if last else total, FF), bf16),
        ]
        + ([pltpu.HBM((wide, HALF), bf16)] * 2 if last else [pltpu.HBM((total, D), bf16)]),
        scratch_shapes=[pltpu.VMEM((wide, D), bf16), pltpu.VMEM((wide, FF), bf16)]
        + [pltpu.VMEM((units, UNIT, FF), bf16)] * 4
        + [
            pltpu.VMEM((min(2, FF // FT), tall, FT), f32),
            pltpu.VMEM((min(2, FF // FT), tall, FT), f32),
            pltpu.VMEM((tall, 128), f32),
            pltpu.VMEM((units, 8, UNIT), f32),
            pltpu.SemaphoreType.DMA((units, 2)),
            pltpu.SemaphoreType.DMA((FF // FT, units, 2)),
            pltpu.SemaphoreType.DMA((units,)),
            pltpu.SemaphoreType.DMA((FF // FT,)),
            pltpu.SemaphoreType.DMA((2,)),
        ],
        input_output_aliases=aliases,
        cost_estimate=pl.CostEstimate(
            flops=200_000_000_000 if last else 1, bytes_accessed=1, transcendentals=0
        ),
        compiler_params=pltpu.CompilerParams(vmem_limit_bytes=(6 * units + 4) * MIB),
    )(*operands)
    return out


def wgrad_kernel(pairs, sums_n, outs_n, *refs):
    hids, ys, refs = refs[:pairs], refs[pairs : 2 * pairs], refs[2 * pairs :]
    sums, outs, refs = refs[:sums_n], refs[sums_n : sums_n + outs_n], refs[sums_n + outs_n :]
    held_s, sem = refs[:pairs], refs[pairs]
    step, steps = pl.program_id(0), HALF // NTILE
    copies = [
        pltpu.make_async_copy(h, s, sem.at[i]) for i, (h, s) in enumerate(zip(hids, held_s))
    ]

    @pl.when(step == 0)
    def _():
        for copy in copies:
            copy.start()

    total = None
    for copy, hid, y in zip(copies, held_s, ys):

        @pl.when(step == 0)
        def _():
            copy.wait()

        part = lax.dot_general(hid[...], y[...], TN, preferred_element_type=jnp.float32)
        total = part if total is None else total + part
    for s in sums:
        total += s[...].astype(jnp.float32)
    if outs_n == 1:
        outs[0][...] = total.astype(outs[0].dtype)
    else:

        @pl.when(step < steps)
        def _():
            outs[1][...] = total.astype(outs[1].dtype)

        @pl.when(step >= steps)
        def _():
            outs[0][...] = total.astype(outs[0].dtype)


def run_wgrad(hids, ys, sums, halves):
    anywhere = pl.BlockSpec(memory_space=pl.ANY)
    steps = HALF // NTILE
    tile = pl.BlockSpec((FF, NTILE), lambda n: (0, n))
    specs, cols = [tile], lambda n: n
    if halves == 2:
        cols = lambda n: lax.rem(n + steps, 2 * steps)
        specs = [
            pl.BlockSpec((FF, NTILE), lambda n: (0, jnp.maximum(n - steps, 0))),
            pl.BlockSpec((FF, NTILE), lambda n: (0, jnp.minimum(n, steps - 1))),
        ]
    return pl.pallas_call(
        functools.partial(wgrad_kernel, len(hids), len(sums), halves),
        grid=(halves * steps,),
        in_specs=[anywhere] * len(hids)
        + [pl.BlockSpec((y.shape[0], NTILE), lambda n: (0, cols(n))) for y in ys]
        + [tile] * len(sums),
        out_specs=specs,
        out_shape=[pltpu.HBM((FF, HALF), jnp.bfloat16)] * halves,
        scratch_shapes=[pltpu.VMEM(h.shape, jnp.bfloat16) for h in hids]
        + [pltpu.SemaphoreType.DMA((len(hids),))],
        cost_estimate=pl.CostEstimate(flops=1, bytes_accessed=1, transcendentals=0),
        compiler_params=pltpu.CompilerParams(vmem_limit_bytes=30 * MIB),
    )(*hids, *ys, *map(outside, sums))


def keep_kernel(source, out, sem):
    copy = pltpu.make_async_copy(source, out, sem)
    copy.start()
    copy.wait()


def keep(array):
    return pl.pallas_call(
        keep_kernel,
        in_specs=[pl.BlockSpec(memory_space=pltpu.HBM)],
        out_specs=pl.BlockSpec(memory_space=pltpu.VMEM),
        out_shape=jax.ShapeDtypeStruct(array.shape, array.dtype),
        scratch_shapes=[pltpu.SemaphoreType.DMA],
        cost_estimate=pl.CostEstimate(flops=1, bytes_accessed=1, transcendentals=0),
        compiler_params=pltpu.CompilerParams(vmem_limit_bytes=8 * MIB),
    )(outside(array))


def local(grad_out, expert_ids, gate_probs, keep_mask, pre_gate, pre_up, w_down):
    dp = lax.axis_index("dp")
    expert = lax.axis_index("expert")
    etp = lax.axis_index("etp")
    x_lo, z = expert // 4, expert % 4
    x_hi, y = etp // 4, etp % 4
    x = x_hi * 2 + x_lo
    turned_y = (y - dp) % 4
    pair = turned_y // 2

    par_x = move(grad_out, near_pair)
    own_w = w_down[0]
    oth_w = move(own_w, other_core)
    kept = gate_probs * keep_mask.astype(jnp.bfloat16)
    meta = jnp.concatenate(
        [
            expert_ids.T.astype(jnp.float32),
            kept.T.astype(jnp.float32),
            jnp.zeros((4, TOK), jnp.float32),
        ],
        axis=0,
    )
    par_meta = move(meta, near_pair)
    kept_w = keep(own_w)
    weights = held(kept_w), held(oth_w)

    sp = jnp.stack([z, x_lo, turned_y % 2]).astype(jnp.int32)
    same0, other0, s1, s2, s3, slots = build_slots(sp, meta, par_meta, grad_out, after(par_x, oth_w, kept_w))

    def place(away_x, away_z):
        source_x, source_z = (x + away_x) % 4, (z + away_z) % 4
        return ((source_x % 2) * 4 + source_z) * 2 + source_x // 2

    common = [pair * PAIR, (1 - pair) * PAIR, dp, dp * HALF, (1 - dp) * HALF]

    def scalars(places):
        return jnp.stack(common + places).astype(jnp.int32)

    cat = lambda *parts: jnp.concatenate(parts, axis=0)
    gate, up = outside(pre_gate[0]), outside(pre_up[0])

    z1 = move(s1, along_z(1))
    z3 = move(s3, along_z(-1))
    n0l = move(other0, along_x(1))
    n0r = move(other0, along_x(-1))
    o0 = move(after(same0, n0l, n0r), along_x(2))
    own0 = cat(same0, n0l, n0r)
    par0 = move(own0, far_pair)

    z1, z3, o0 = lax.optimization_barrier((z1, z3, o0))
    o13 = cat(z1[:PAIR], z3[:PAIR])
    n13 = cat(z1[PAIR:], z3[PAIR:])
    own1 = [o0, o13]
    par1 = [move(v, far_pair) for v in own1]
    n13l = move(n13, along_x(1))
    n13r = move(n13, along_x(-1))
    z2 = move(after(s2, z1, z3), along_z(2))

    size_a, size_b, size_c = 2 * padded(3 * PAIR), 2 * (padded(PAIR) + 2 * PAIR), 8 * PAIR
    total = size_a + size_b + size_c
    sp_a = scalars([place(0, 0), place(-1, 0), place(1, 0)])
    rows_a = [own0, par0]
    filled = run_act((3,), sp_a, rows_a, weights, gate, up, None, 0, total)

    n13l, n13r, z2, par1[0] = lax.optimization_barrier(
        (n13l, n13r, z2, par1[0], filled[3])
    )[:4]
    same2, other2 = z2[:PAIR], z2[PAIR:]
    own2 = [n13l, n13r]
    par2 = [move(v, far_pair) for v in own2]
    o13r = move(after(o13, n13l), along_x(2))
    n2l = move(other2, along_x(1))
    n2r = move(other2, along_x(-1))

    sp_b = scalars([place(2, 0), place(0, -1), place(0, 1)])
    rows_b = [own1[0], par1[0], own1[1], par1[1]]
    filled = run_act((1, 2), sp_b, rows_b, weights, gate, up, filled, size_a, total)

    o13r, same2 = lax.optimization_barrier((o13r, same2, filled[3]))[:2]
    own3 = [o13r, same2]
    par3 = [move(v, far_pair) for v in own3]
    o2 = move(same2, along_x(2))
    sp_c = scalars([place(-1, -1), place(-1, 1), place(1, -1), place(1, 1)])
    rows_c = [own2[0], par2[0], own2[1], par2[1]]
    filled = run_act((2, 2), sp_c, rows_c, weights, gate, up, filled, size_a + size_b, total)

    n2l, n2r, par3[1] = lax.optimization_barrier((n2l, n2r, par3[1], filled[3]))[:3]
    own4 = [n2l, n2r]
    par4 = [move(v, far_pair) for v in own4]
    own_sum, oth_sum = run_wgrad([outside(filled[3])], [outside(filled[4])], [], 2)
    far_sum = move(oth_sum, other_core)
    own5 = o2
    par5 = after(move(own5, far_pair), own_sum)

    sp_d = scalars(
        [place(2, -1), place(2, 1), place(0, 2), place(-1, 2), place(1, 2), place(2, 2)]
    )
    late = [own3[0], par3[0], own3[1], par3[1], own4[0], par4[0], own4[1], par4[1], own5, par5]
    grad_gate, grad_up, term, hid_d, mine_d, far_d = run_act(
        (2, 1, 1, 1, 1), sp_d, late, weights, gate, up, filled[:3]
    )
    far_rows, far_hid = move(far_d, other_core), move(hid_d, other_core)
    returned = lax.all_to_all(
        term[:, 0, :].reshape(64, CAP), ("expert", "etp"), split_axis=0, concat_axis=0, tiled=True
    )
    (grad_w,) = run_wgrad(
        [outside(hid_d), far_hid], [outside(mine_d), far_rows], [own_sum, far_sum], 1
    )
    returned, grad_w = lax.optimization_barrier((returned, grad_w))

    summed = returned.reshape(EXPERTS, 8, CAP).sum(axis=1)
    hit = (expert_ids.T[:, :, None, None] == jnp.arange(EXPERTS)[None, None, :, None]) & (
        slots[:2, :, None, None] == jnp.arange(CAP, dtype=jnp.float32)[None, None, None, :]
    )
    picked = jnp.sum(jnp.where(hit, summed[None, None], 0.0), axis=(2, 3)).T
    kept_only = keep_mask.astype(jnp.float32) * picked
    grad_gate_probs = kept_only / gate_probs.astype(jnp.float32)
    return (grad_gate[None], grad_up[None], grad_w[None], grad_gate_probs)


def solution(mesh):
    tokens = P(("dp", "expert", "etp"), None)
    acts = P("expert", "dp", "etp")
    weight = P("expert", "etp", "dp")
    return jax.shard_map(
        local,
        mesh=mesh,
        in_specs=(tokens, tokens, tokens, tokens, acts, acts, weight),
        out_specs=(acts, acts, weight, tokens),
        check_vma=False,
    )
```

```python
import functools

import jax
import jax.numpy as jnp
from jax import lax
from jax.experimental import pallas as pl
from jax.experimental.pallas import tpu as pltpu
from jax.sharding import PartitionSpec as P

AXES = ("dp", "expert", "etp")
EXPERTS = 8
CAP = 36
TOK = 128
D = 3072
HALF = 1536
FF = 1024
ROWS = 2304
PAIR = 2 * CAP
UNIT = 4 * CAP
FT = 1024
NTILE = 512
MIB = 1024 * 1024
NT = (((1,), (1,)), ((), ()))
TN = (((0,), (0,)), ((), ()))


def position(flat):
    dp, rest = divmod(flat, 64)
    expert, etp = divmod(rest, 8)
    x_lo, z = divmod(expert, 4)
    x_hi, y = divmod(etp, 4)
    return dp, x_hi * 2 + x_lo, y, z


def flat_of(dp, x, y, z):
    return dp * 64 + ((x % 2) * 4 + z) * 8 + (x // 2) * 4 + y


def move(array, step):
    pairs = []
    for source in range(128):
        dp, x, y, z = position(source)
        pairs.append((source, flat_of(*step(dp, x, y, z))))
    return lax.ppermute(array, AXES, pairs)


def along_x(k):
    return lambda dp, x, y, z: (dp, (x + k) % 4, y, z)


def along_z(k):
    return lambda dp, x, y, z: (dp, x, y, (z + k) % 4)


def turned(dp, y, change):
    return (change((y - dp) % 4) + dp) % 4


def near_pair(dp, x, y, z):
    return dp, x, turned(dp, y, lambda v: v ^ 1), z


def far_pair(dp, x, y, z):
    return dp, x, turned(dp, y, lambda v: 3 - v), z


def other_core(dp, x, y, z):
    return 1 - dp, x, y, z


def after(value, *others):
    return lax.optimization_barrier((value,) + others)[0]


def held(array):
    return pltpu.with_memory_space_constraint(array, pltpu.VMEM)


def outside(array):
    return pltpu.with_memory_space_constraint(array, pltpu.HBM)


def slot_lines(meta):
    names = lax.broadcasted_iota(jnp.int32, (EXPERTS, TOK), 0).astype(jnp.float32)
    first = (names == meta[0:1, :]).astype(jnp.float32)
    second = (names == meta[1:2, :]).astype(jnp.float32)
    row = lax.broadcasted_iota(jnp.int32, (TOK, TOK), 0)
    col = lax.broadcasted_iota(jnp.int32, (TOK, TOK), 1)
    earlier = (row < col).astype(jnp.bfloat16)
    before = jnp.dot(
        (first + second).astype(jnp.bfloat16), earlier, preferred_element_type=jnp.float32
    )
    return (
        jnp.sum(before * first, axis=0, keepdims=True),
        jnp.sum(before * second, axis=0, keepdims=True),
    )


def slots_kernel(sp, own_meta, par_meta, own_x, par_x, *refs):
    outs, both = refs[:-1], refs[-1]
    both[:TOK, :] = own_x[...]
    both[TOK:, :] = par_x[...]
    z, x_lo, odd = sp[0], sp[1], sp[2]
    own_slots = slot_lines(own_meta[...])
    par_slots = slot_lines(par_meta[...])
    outs[-1][...] = jnp.concatenate(
        [own_slots[0], own_slots[1], jnp.zeros((6, TOK), jnp.float32)], axis=0
    )
    row = lax.broadcasted_iota(jnp.int32, (UNIT, 1), 0)
    other = row >= PAIR
    within = jnp.where(other, row - PAIR, row)
    late = (within >= CAP).astype(jnp.int32)
    slot = jnp.where(within >= CAP, within - CAP, within).astype(jnp.float32)
    lo = jnp.where(other, 1 - x_lo, x_lo)
    picks = []
    for mine, meta, slots in ((True, own_meta, own_slots), (False, par_meta, par_slots)):
        here = late == (odd if mine else 1 - odd)
        rows = []
        for k in range(4):
            expert = (lo * 4 + lax.rem(z + k, 4)).astype(jnp.float32)
            pick = jnp.zeros((UNIT, TOK), jnp.float32)
            for j in range(2):
                hit = (meta[j : j + 1, :] == expert) & (slots[j] == slot) & here
                pick = pick + jnp.where(hit, meta[2 + j : 3 + j, :], 0.0)
            rows.append(pick)
        picks.append(jnp.concatenate(rows, axis=0).astype(jnp.bfloat16))
    pick = jnp.concatenate(picks, axis=1)
    step = 512
    for at in range(0, D, step):
        cols = slice(at, at + step)
        total = jnp.dot(pick, both[:, cols], preferred_element_type=jnp.float32)
        total = total.astype(jnp.bfloat16)
        at = 0
        for out in outs[:-1]:
            out[:, cols] = total[at : at + out.shape[0]]
            at += out.shape[0]


def build_slots(sp, own_meta, par_meta, own_x, par_x):
    vmem = pl.BlockSpec(memory_space=pltpu.VMEM)
    return pl.pallas_call(
        slots_kernel,
        in_specs=[pl.BlockSpec(memory_space=pltpu.SMEM)] + [vmem] * 4,
        out_specs=[vmem] * 6,
        out_shape=[
            jax.ShapeDtypeStruct((rows, D), jnp.bfloat16)
            for rows in (PAIR, PAIR, UNIT, UNIT, UNIT)
        ]
        + [jax.ShapeDtypeStruct((8, TOK), jnp.float32)],
        scratch_shapes=[pltpu.VMEM((2 * TOK, D), jnp.bfloat16)],
        cost_estimate=pl.CostEstimate(flops=1, bytes_accessed=1, transcendentals=0),
        compiler_params=pltpu.CompilerParams(vmem_limit_bytes=16 * MIB),
    )(sp, own_meta, par_meta, held(own_x), held(par_x))


def padded(rows):
    return (rows + 15) // 16 * 16


def act_kernel(sizes, offset, first, last, sp, *refs):
    units = sum(sizes)
    ys, refs = refs[: 2 * len(sizes)], refs[2 * len(sizes) :]
    w_halves, gate, up, refs = refs[:2], refs[2], refs[3], refs[4:]
    if not first:
        refs = refs[3 if last else 5 :]
    grad_gate, grad_up, term, hid_out = refs[:4]
    rows_outs, refs = (refs[4:6], refs[6:]) if last else (refs[4:5], refs[5:])
    rows_s, hid, gate_s, up_s, ggate_s, gup_s, back_s, hid_s, sum_s, term_s = refs[:10]
    sem_in, sem_out, sem_t, sem_h, sem_r = refs[10:]
    places = [pl.multiple_of(sp[5 + i] * UNIT, UNIT) for i in range(units)]
    loads = []
    for i in range(units):
        rows = pl.ds(places[i], UNIT)
        loads.append(
            (
                pltpu.make_async_copy(gate.at[rows, :], gate_s.at[i], sem_in.at[i, 0]),
                pltpu.make_async_copy(up.at[rows, :], up_s.at[i], sem_in.at[i, 1]),
            )
        )
    for pair in loads:
        for copy in pair:
            copy.start()
    starts, at = [], 0
    for n, y in enumerate(ys):
        rows = y.shape[0]
        starts.append(at)
        for h in range(2):
            cols = pl.ds(pl.multiple_of(sp[3 + h], 128), HALF)
            rows_s[at : at + rows, h * HALF : (h + 1) * HALF] = y[:, cols]
        gap = padded(rows) - rows
        if gap:
            rows_s[at + rows : at + rows + gap, :] = jnp.zeros((gap, D), jnp.bfloat16)
        at += rows + gap
    turn = sp[2] > 0
    wide = pl.ds(offset, rows_s.shape[0])
    if last:
        stores = [
            pltpu.make_async_copy(rows_s.at[:, pl.ds(n * HALF, HALF)], out, sem_r.at[n])
            for n, out in enumerate(rows_outs)
        ]
    else:
        stores = [pltpu.make_async_copy(rows_s, rows_outs[0].at[wide, :], sem_r.at[0])]
    for copy in stores:
        copy.start()

    def back_of(f):
        cols = pl.ds(f * FT, FT)
        return lax.dot_general(
            rows_s[:, :HALF], w_halves[0][cols, :], NT, preferred_element_type=jnp.float32
        ) + lax.dot_general(
            rows_s[:, HALF:], w_halves[1][cols, :], NT, preferred_element_type=jnp.float32
        )

    later = back_of(0)
    for f in range(FF // FT):
        cols = pl.ds(f * FT, FT)
        back_f, hid_f = back_s.at[f % back_s.shape[0]], hid_s.at[f % hid_s.shape[0]]
        back = later
        base = 0
        for g, size in enumerate(sizes):
            for side in range(2):
                for j in range(size):
                    start = pl.multiple_of((base + j) * UNIT + sp[side], 8)
                    piece = starts[2 * g + side] + j * PAIR
                    back_f[pl.ds(start, PAIR), :] = back[piece : piece + PAIR]
            base += size
        if f + 1 < FF // FT:
            later = back_of(f + 1)
        for i in range(units):
            rows = pl.ds(i * UNIT, UNIT)
            if f == 0:
                for copy in loads[i]:
                    copy.wait()
            straight = back_f[rows, :]
            upstream = jnp.where(turn, pltpu.roll(straight, CAP, 0), straight)
            a = gate_s[i, :, cols].astype(jnp.float32)
            b = up_s[i, :, cols].astype(jnp.float32)
            s = 0.5 * jnp.tanh(0.5 * a) + 0.5
            swish = a * s
            product = swish * b
            scaled = upstream * b
            ggate_s[i, :, cols] = (scaled * (s + swish * (1.0 - s))).astype(jnp.bfloat16)
            gup_s[i, :, cols] = (upstream * swish).astype(jnp.bfloat16)
            here = swish * scaled
            here = sum(here[:, c : c + 128] for c in range(0, FT, 128))
            if f == 0:
                sum_s[rows, :] = here
            else:
                sum_s[rows, :] += here
            hid_f[rows, :] = jnp.where(turn, pltpu.roll(product, UNIT - CAP, 0), product)
            for n, (src, dst) in enumerate(((ggate_s, grad_gate), (gup_s, grad_up))):
                copy = pltpu.make_async_copy(
                    src.at[i, :, cols],
                    dst.at[pl.ds(places[i], UNIT), cols],
                    sem_out.at[f, i, n],
                )
                copy.start()
                stores.append(copy)
        pieces, base = [], 0
        for size in sizes:
            for side in range(2):
                for j in range(size):
                    start = pl.multiple_of((base + j) * UNIT + sp[side], 8)
                    pieces.append(hid_f[pl.ds(start, PAIR), :])
                gap = padded(size * PAIR) - size * PAIR
                if gap:
                    pieces.append(jnp.zeros((gap, FT), jnp.float32))
            base += size
        hid[:, cols] = jnp.concatenate(pieces, axis=0).astype(jnp.bfloat16)
        copy = pltpu.make_async_copy(hid.at[:, cols], hid_out.at[wide, cols], sem_h.at[f])
        copy.start()
        stores.append(copy)
    ones = jnp.ones((8, 128), jnp.float32)
    for i in range(units):
        term_s[i] = lax.dot_general(
            ones,
            sum_s[pl.ds(i * UNIT, UNIT), :],
            NT,
            precision=lax.Precision.HIGHEST,
            preferred_element_type=jnp.float32,
        )[0:1]
        copy = pltpu.make_async_copy(term_s.at[i], term.at[sp[5 + i]], sem_t.at[i])
        copy.start()
        stores.append(copy)
    for copy in stores:
        copy.wait()


def run_act(sizes, sp, ys, weights, gate, up, carried, offset=0, total=None):
    units = sum(sizes)
    vmem = pl.BlockSpec(memory_space=pltpu.VMEM)
    anywhere = pl.BlockSpec(memory_space=pltpu.HBM)
    first, last = carried is None, total is None
    in_specs = [pl.BlockSpec(memory_space=pltpu.SMEM)] + [vmem] * (len(ys) + 2) + [anywhere] * 2
    operands = [sp] + [y if first else held(y) for y in ys] + list(weights) + [gate, up]
    aliases = {}
    if not first:
        at = len(operands)
        in_specs += [anywhere] * len(carried)
        operands += list(carried)
        aliases = {at + n: n for n in range(len(carried))}
    bf16, f32 = jnp.bfloat16, jnp.float32
    tall = units * UNIT
    wide = sum(padded(y.shape[0]) for y in ys)
    out = pl.pallas_call(
        functools.partial(act_kernel, sizes, offset, first, last),
        in_specs=in_specs,
        out_specs=[anywhere] * (6 if last else 5),
        out_shape=[
            pltpu.HBM((ROWS, FF), bf16),
            pltpu.HBM((ROWS, FF), bf16),
            pltpu.HBM((16, 1, UNIT), f32),
            pltpu.HBM((wide if last else total, FF), bf16),
        ]
        + ([pltpu.HBM((wide, HALF), bf16)] * 2 if last else [pltpu.HBM((total, D), bf16)]),
        scratch_shapes=[pltpu.VMEM((wide, D), bf16), pltpu.VMEM((wide, FF), bf16)]
        + [pltpu.VMEM((units, UNIT, FF), bf16)] * 4
        + [
            pltpu.VMEM((min(2, FF // FT), tall, FT), f32),
            pltpu.VMEM((min(2, FF // FT), tall, FT), f32),
            pltpu.VMEM((tall, 128), f32),
            pltpu.VMEM((units, 1, UNIT), f32),
            pltpu.SemaphoreType.DMA((units, 2)),
            pltpu.SemaphoreType.DMA((FF // FT, units, 2)),
            pltpu.SemaphoreType.DMA((units,)),
            pltpu.SemaphoreType.DMA((FF // FT,)),
            pltpu.SemaphoreType.DMA((2,)),
        ],
        input_output_aliases=aliases,
        cost_estimate=pl.CostEstimate(
            flops=200_000_000_000 if last else 1, bytes_accessed=1, transcendentals=0
        ),
        compiler_params=pltpu.CompilerParams(vmem_limit_bytes=(6 * units + 4) * MIB),
    )(*operands)
    return out


def wgrad_kernel(pairs, sums_n, outs_n, *refs):
    hids, ys, refs = refs[:pairs], refs[pairs : 2 * pairs], refs[2 * pairs :]
    sums, outs, refs = refs[:sums_n], refs[sums_n : sums_n + outs_n], refs[sums_n + outs_n :]
    held_s, sem = refs[:pairs], refs[pairs]
    step, steps = pl.program_id(0), HALF // NTILE
    copies = [
        pltpu.make_async_copy(h, s, sem.at[i]) for i, (h, s) in enumerate(zip(hids, held_s))
    ]

    @pl.when(step == 0)
    def _():
        for copy in copies:
            copy.start()

    total = None
    for copy, hid, y in zip(copies, held_s, ys):

        @pl.when(step == 0)
        def _():
            copy.wait()

        part = lax.dot_general(hid[...], y[...], TN, preferred_element_type=jnp.float32)
        total = part if total is None else total + part
    for s in sums:
        total += s[...].astype(jnp.float32)
    if outs_n == 1:
        outs[0][...] = total.astype(outs[0].dtype)
    else:

        @pl.when(step < steps)
        def _():
            outs[1][...] = total.astype(outs[1].dtype)

        @pl.when(step >= steps)
        def _():
            outs[0][...] = total.astype(outs[0].dtype)


def run_wgrad(hids, ys, sums, halves):
    anywhere = pl.BlockSpec(memory_space=pl.ANY)
    steps = HALF // NTILE
    tile = pl.BlockSpec((FF, NTILE), lambda n: (0, n))
    specs, cols = [tile], lambda n: n
    if halves == 2:
        cols = lambda n: lax.rem(n + steps, 2 * steps)
        specs = [
            pl.BlockSpec((FF, NTILE), lambda n: (0, jnp.maximum(n - steps, 0))),
            pl.BlockSpec((FF, NTILE), lambda n: (0, jnp.minimum(n, steps - 1))),
        ]
    return pl.pallas_call(
        functools.partial(wgrad_kernel, len(hids), len(sums), halves),
        grid=(halves * steps,),
        in_specs=[anywhere] * len(hids)
        + [pl.BlockSpec((y.shape[0], NTILE), lambda n: (0, cols(n))) for y in ys]
        + [tile] * len(sums),
        out_specs=specs,
        out_shape=[pltpu.HBM((FF, HALF), jnp.bfloat16)] * halves,
        scratch_shapes=[pltpu.VMEM(h.shape, jnp.bfloat16) for h in hids]
        + [pltpu.SemaphoreType.DMA((len(hids),))],
        cost_estimate=pl.CostEstimate(flops=1, bytes_accessed=1, transcendentals=0),
        compiler_params=pltpu.CompilerParams(vmem_limit_bytes=30 * MIB),
    )(*hids, *ys, *map(outside, sums))


def keep_kernel(source, out, sem):
    copy = pltpu.make_async_copy(source, out, sem)
    copy.start()
    copy.wait()


def keep(array):
    return pl.pallas_call(
        keep_kernel,
        in_specs=[pl.BlockSpec(memory_space=pltpu.HBM)],
        out_specs=pl.BlockSpec(memory_space=pltpu.VMEM),
        out_shape=jax.ShapeDtypeStruct(array.shape, array.dtype),
        scratch_shapes=[pltpu.SemaphoreType.DMA],
        cost_estimate=pl.CostEstimate(flops=1, bytes_accessed=1, transcendentals=0),
        compiler_params=pltpu.CompilerParams(vmem_limit_bytes=8 * MIB),
    )(outside(array))


def local(grad_out, expert_ids, gate_probs, keep_mask, pre_gate, pre_up, w_down):
    dp = lax.axis_index("dp")
    expert = lax.axis_index("expert")
    etp = lax.axis_index("etp")
    x_lo, z = expert // 4, expert % 4
    x_hi, y = etp // 4, etp % 4
    x = x_hi * 2 + x_lo
    turned_y = (y - dp) % 4
    pair = turned_y // 2

    par_x = move(grad_out, near_pair)
    own_w = w_down[0]
    kept = gate_probs * keep_mask.astype(jnp.bfloat16)
    meta = jnp.concatenate(
        [
            expert_ids.T.astype(jnp.float32),
            kept.T.astype(jnp.float32),
            jnp.zeros((4, TOK), jnp.float32),
        ],
        axis=0,
    )
    par_meta = move(meta, near_pair)
    kept_w = keep(own_w)
    oth_w = move(after(own_w, par_x, par_meta, kept_w), other_core)
    weights = held(kept_w), held(oth_w)

    sp = jnp.stack([z, x_lo, turned_y % 2]).astype(jnp.int32)
    same0, other0, s1, s2, s3, slots = build_slots(sp, meta, par_meta, grad_out, after(par_x, kept_w))

    def place(away_x, away_z):
        source_x, source_z = (x + away_x) % 4, (z + away_z) % 4
        return ((source_x % 2) * 4 + source_z) * 2 + source_x // 2

    common = [pair * PAIR, (1 - pair) * PAIR, dp, dp * HALF, (1 - dp) * HALF]

    def scalars(places):
        return jnp.stack(common + places).astype(jnp.int32)

    cat = lambda *parts: jnp.concatenate(parts, axis=0)
    gate, up = outside(pre_gate[0]), outside(pre_up[0])

    z1 = move(s1, along_z(1))
    z3 = move(s3, along_z(-1))
    n0l = move(other0, along_x(1))
    n0r = move(other0, along_x(-1))
    o0 = move(after(same0, n0l, n0r), along_x(2))
    own0 = cat(same0, n0l, n0r)
    par0 = move(own0, far_pair)

    z1, z3, o0 = lax.optimization_barrier((z1, z3, o0))
    o13 = cat(z1[:PAIR], z3[:PAIR])
    n13 = cat(z1[PAIR:], z3[PAIR:])
    own1 = [o0, o13]
    par1 = [move(v, far_pair) for v in own1]
    n13l = move(n13, along_x(1))
    n13r = move(n13, along_x(-1))
    z2 = move(after(s2, z1, z3), along_z(2))

    size_a, size_b, size_c = 2 * padded(3 * PAIR), 2 * (padded(PAIR) + 2 * PAIR), 8 * PAIR
    total = size_a + size_b + size_c
    sp_a = scalars([place(0, 0), place(-1, 0), place(1, 0)])
    rows_a = [own0, par0]
    filled = run_act((3,), sp_a, rows_a, weights, gate, up, None, 0, total)

    n13l, n13r, z2, par1[0] = lax.optimization_barrier(
        (n13l, n13r, z2, par1[0], filled[3])
    )[:4]
    same2, other2 = z2[:PAIR], z2[PAIR:]
    own2 = [n13l, n13r]
    par2 = [move(v, far_pair) for v in own2]
    o13r = move(after(o13, n13l), along_x(2))
    n2l = move(other2, along_x(1))
    n2r = move(other2, along_x(-1))

    sp_b = scalars([place(2, 0), place(0, -1), place(0, 1)])
    rows_b = [own1[0], par1[0], own1[1], par1[1]]
    filled = run_act((1, 2), sp_b, rows_b, weights, gate, up, filled, size_a, total)

    o13r, same2 = lax.optimization_barrier((o13r, same2, filled[3]))[:2]
    own3 = [o13r, same2]
    par3 = [move(v, far_pair) for v in own3]
    o2 = move(same2, along_x(2))
    sp_c = scalars([place(-1, -1), place(-1, 1), place(1, -1), place(1, 1)])
    rows_c = [own2[0], par2[0], own2[1], par2[1]]
    filled = run_act((2, 2), sp_c, rows_c, weights, gate, up, filled, size_a + size_b, total)

    n2l, n2r, par3[1] = lax.optimization_barrier((n2l, n2r, par3[1], filled[3]))[:3]
    own4 = [n2l, n2r]
    par4 = [move(v, far_pair) for v in own4]
    own_sum, oth_sum = run_wgrad([outside(filled[3])], [outside(filled[4])], [], 2)
    far_sum = move(oth_sum, other_core)
    own5 = o2
    par5 = after(move(own5, far_pair), own_sum)

    sp_d = scalars(
        [place(2, -1), place(2, 1), place(0, 2), place(-1, 2), place(1, 2), place(2, 2)]
    )
    late = [own3[0], par3[0], own3[1], par3[1], own4[0], par4[0], own4[1], par4[1], own5, par5]
    grad_gate, grad_up, term, hid_d, mine_d, far_d = run_act(
        (2, 1, 1, 1, 1), sp_d, late, weights, gate, up, filled[:3]
    )
    far_rows, far_hid = move(far_d, other_core), move(hid_d, other_core)
    returned = lax.all_to_all(
        term.reshape(64, CAP), ("expert", "etp"), split_axis=0, concat_axis=0, tiled=True
    )
    (grad_w,) = run_wgrad(
        [outside(hid_d), far_hid], [outside(mine_d), far_rows], [own_sum, far_sum], 1
    )
    returned, grad_w = lax.optimization_barrier((returned, grad_w))

    summed = returned.reshape(EXPERTS, 8, CAP).sum(axis=1)
    hit = (expert_ids.T[:, :, None, None] == jnp.arange(EXPERTS)[None, None, :, None]) & (
        slots[:2, :, None, None] == jnp.arange(CAP, dtype=jnp.float32)[None, None, None, :]
    )
    picked = jnp.sum(jnp.where(hit, summed[None, None], 0.0), axis=(2, 3)).T
    kept_only = keep_mask.astype(jnp.float32) * picked
    grad_gate_probs = kept_only / gate_probs.astype(jnp.float32)
    return (grad_gate[None], grad_up[None], grad_w[None], grad_gate_probs)


def solution(mesh):
    tokens = P(("dp", "expert", "etp"), None)
    acts = P("expert", "dp", "etp")
    weight = P("expert", "etp", "dp")
    return jax.shard_map(
        local,
        mesh=mesh,
        in_specs=(tokens, tokens, tokens, tokens, acts, acts, weight),
        out_specs=(acts, acts, weight, tokens),
        check_vma=False,
    )
```
